512 devices in a mesh: scen: 16 (over z_hi, y, core), node: 32 (over x, z_lo).
Axes of the slice: x: 4, y: 4, z: 16 (z_hi: 2, z_lo: 8; z = z_hi * 8 + z_lo), core: 2. Of those that a mesh axis runs over, the one named last changes fastest.
Arguments:
- factors: bfloat16 [32, 16, 1024, 1024], P('node', 'scen'), may hold values from -0.1875 to 0.1875
- couple: bfloat16 [32, 16, 1024, 512], P('node', 'scen'), may hold values from -0.1875 to 0.1875
- leaf_rhs: bfloat16 [32, 16, 2, 1024], P('node', 'scen'), may hold values from -6 to 6
- node_diag: float32 [32, 512, 512], P('node', 'scen'), as said below
- node_rhs: float32 [32, 2, 512], P('node', None, 'scen'), may hold values from -6 to 6
- link_root: float32 [32, 512, 512], P('node', 'scen'), may hold values from -1.5 to 1.5
- root_diag: float32 [512, 512], replicated, as said below
- root_rhs: float32 [2, 512], replicated, may hold values from -6 to 6
Outputs:
- leaf_solution: float32 [32, 16, 2, 1024], P('node', 'scen')
- node_solution: float32 [32, 2, 512], P('node', None, 'scen')
- root_solution: float32 [2, 512], replicated
The draws below stay inside these ranges and needn't reach their ends.
Inputs may be any that keep to these rules, and one draw needn't show every extreme that they name: `node_diag`: symmetric positive definite. `root_diag`: symmetric positive definite.
All inputs are finite; a program needn't handle non-finite values.
Results may differ from the reference program's by a relative error of at most 0.0036.
Values sent between devices are 32-bit elements; how exact they have to be, the bound alone decides.
A program may use at most 64 MiB of HBM per device.

```python
import jax
import jax.numpy as jnp
from jax import lax

KO = 1024
LINK = 512
NODES = 32
SUB = 16


def definite(key, count, order, lower_eig, upper_eig):
    first, second = jax.random.split(jax.random.fold_in(key, 11))
    columns = 2 * order
    basis = jax.random.normal(first, (count, order, columns), jnp.float32)
    levels = jnp.exp(jax.random.uniform(second, (count, columns), jnp.float32, jnp.log(lower_eig), jnp.log(upper_eig)))
    weighted = basis * levels[:, None, :]
    product = jnp.einsum('nik,njk->nij', weighted, basis, precision=lax.Precision.HIGHEST) / columns
    return 0.5 * (product + jnp.swapaxes(product, 1, 2))


def draw_node_diag(key, part):
    return definite(key, NODES, LINK, 1.0, 4000.0)


def draw_root_diag(key, part):
    return definite(key, 1, LINK, 2.0, 8000.0)[0]


def shard_levels(rng, dims, shards, smallest, largest):
    gain, own = 1.0, jax.random.fold_in(rng, 6)
    for position, shards_of in shards:
        steps = jnp.exp(jax.random.uniform(jax.random.fold_in(own, position), (shards_of,), jnp.float32, smallest / len(shards), largest / len(shards)))
        gain = gain * jnp.repeat(steps, dims[position] // shards_of).reshape([-1 if axis == position else 1 for axis in range(len(dims))])
    return gain


def centred(rng, shape, deviation, most, pieces=(), kind=jnp.bfloat16):
    array = jax.random.normal(rng, shape, jnp.float32) * deviation
    if len(pieces) > 0:
        array = shard_levels(rng, shape, pieces, -0.22, 0.18) * array
    return jnp.clip(array, min=-most, max=most).astype(kind)


def setup_inputs(seed: int = 0) -> dict:
    key_of = jax.random.split(jax.random.key(seed), 9)
    factors = centred(key_of[0], (NODES, SUB, KO, KO), KO ** -0.5, 0.1875, ((0, 32), (1, 16)))
    couple = centred(key_of[1], (NODES, SUB, KO, LINK), KO ** -0.5, 0.1875, ((0, 32), (1, 16)))
    leaf_rhs = centred(key_of[2], (NODES, SUB, 2, KO), 1.0, 6.0, ((0, 32), (1, 16)))
    node_diag = draw_node_diag(jax.random.fold_in(key_of[8], 71), 0)
    node_rhs = centred(key_of[4], (NODES, 2, LINK), 1.0, 6.0, ((0, 32), (2, 16)), jnp.float32)
    link_root = centred(key_of[5], (NODES, LINK, LINK), 16 ** -0.5, 1.5, ((0, 32), (1, 16)), jnp.float32)
    root_diag = draw_root_diag(jax.random.fold_in(key_of[8], 71), 0)
    root_rhs = centred(key_of[7], (2, LINK), 1.0, 6.0, (), jnp.float32)
    return dict(factors=factors, couple=couple, leaf_rhs=leaf_rhs, node_diag=node_diag, node_rhs=node_rhs, link_root=link_root, root_diag=root_diag, root_rhs=root_rhs)


HIGH = lax.Precision.HIGHEST

def leaf_terms(factor, coupling, rights):
    wide_factor = factor.astype(jnp.float32)
    reduced = jnp.dot(wide_factor.T, coupling.astype(jnp.float32), precision=HIGH).astype(jnp.bfloat16)
    projected = jnp.dot(rights.astype(jnp.float32), wide_factor, precision=HIGH)
    wide_reduced = reduced.astype(jnp.float32)
    schur = jnp.dot(wide_reduced.T, wide_reduced, precision=HIGH)
    rounded = lax.optimization_barrier(projected.astype(jnp.bfloat16)).astype(jnp.float32)
    vector = jnp.dot(rounded, wide_reduced, precision=HIGH)
    return (reduced, projected, schur, vector)

def node_section(packed):
    factor_set, coupling_set, rights_set, diag_block, node_vec, root_link = packed
    reduced, projected, schur, vector = jax.vmap(leaf_terms)(factor_set, coupling_set, rights_set)
    node_matrix = diag_block + jnp.sum(schur, axis=0)
    node_vector = node_vec + jnp.sum(vector, axis=0)
    lower = jnp.linalg.cholesky(node_matrix)
    solved_link = jax.scipy.linalg.cho_solve((lower, True), root_link)
    solved_rhs = jax.scipy.linalg.cho_solve((lower, True), node_vector.T)
    root_part = jnp.dot(root_link.T, solved_link, precision=HIGH)
    root_vec = jnp.dot(root_link.T, solved_rhs, precision=HIGH)
    return (lower, node_vector, root_part, root_vec)

def back_section(packed):
    factor_set, coupling_set, rights_set, lower, node_vector, root_link, root_sol = packed
    shifted = node_vector.T - jnp.dot(root_link, root_sol, precision=HIGH)
    node_sol = jax.scipy.linalg.cho_solve((lower, True), shifted)
    node_low = node_sol.astype(jnp.bfloat16).astype(jnp.float32)

    def one_leaf(factor, coupling, rights):
        reduced, projected, schur, vector = leaf_terms(factor, coupling, rights)
        update = jnp.dot(reduced.astype(jnp.float32), node_low, precision=HIGH)
        difference = (update.T - projected).astype(jnp.bfloat16).astype(jnp.float32)
        return jnp.dot(difference, factor.astype(jnp.float32).T, precision=HIGH)
    leaves = jax.vmap(one_leaf)(factor_set, coupling_set, rights_set)
    return (leaves, node_sol.T)

def reference(factors, couple, leaf_rhs, node_diag, node_rhs, link_root, root_diag, root_rhs):
    lowers, vectors, root_parts, root_vecs = lax.map(node_section, (factors, couple, leaf_rhs, node_diag, node_rhs, link_root))
    root_matrix = root_diag + jnp.sum(root_parts, axis=0)
    root_vector = jnp.sum(root_vecs, axis=0) - root_rhs.T
    root_lower = jnp.linalg.cholesky(root_matrix)
    root_sol = jax.scipy.linalg.cho_solve((root_lower, True), root_vector)

    def back_node(packed):
        return back_section(packed + (root_sol,))
    leaves, nodes = lax.map(back_node, (factors, couple, leaf_rhs, lowers, vectors, link_root))
    return (leaves, nodes, root_sol.T)
```

```python
import jax
import jax.numpy as jnp
from jax import lax
from jax.experimental import pallas as pl
from jax.experimental.pallas import tpu as pltpu
from jax.sharding import Mesh
from jax.sharding import PartitionSpec as P

AXES = ("zh", "y", "core", "x", "zl")
MESH = pl.DeviceIdType.MESH
HIGH = lax.Precision.HIGHEST
F32 = jnp.float32
BF16 = jnp.bfloat16


def dot(a, b, dims=((1,), (0,)), precision=None):
    return lax.dot_general(a, b, (dims, ((), ())), precision=precision, preferred_element_type=F32)


def reciprocal(x):
    r = pl.reciprocal(x, approx=True)
    h = 1.0 - x * r
    return r + r * (h + h * h)


def inverse_128(a):
    rows = lax.broadcasted_iota(jnp.int32, (8, 128), 0)
    lanes = lax.broadcasted_iota(jnp.int32, (8, 128), 1)
    wide_lanes = lax.broadcasted_iota(jnp.int32, (128, 128), 1)
    for s in range(16):
        at = 8 * s
        panel = a[at : at + 8]
        cols = jnp.stack([jnp.broadcast_to(panel[:, at + j : at + j + 1], (8, 128)) for j in range(8)])
        here = (lanes >= at) & (lanes < at + 8)
        panel = jnp.where(here, jnp.where(lanes - at == rows, 1.0, 0.0), panel)
        for j in range(8):
            mine = rows == j
            col = cols[0]
            inv = reciprocal(jnp.broadcast_to(col[j : j + 1], (8, 128)))
            f = jnp.where(mine, -inv, col * inv)
            if j < 7:
                rest = cols[1:]
                pivot = jnp.broadcast_to(rest[:, j : j + 1], rest.shape)
                cols = jnp.where(mine[None], 0.0, rest) - f[None] * pivot
            panel = jnp.where(mine, 0.0, panel) - f * jnp.broadcast_to(panel[j : j + 1], (8, 128))
        new = jnp.where((wide_lanes >= at) & (wide_lanes < at + 8), 0.0, a)
        for j in range(8):
            new = new - jnp.broadcast_to(a[:, at + j : at + j + 1], (128, 128)) * jnp.broadcast_to(
                panel[j : j + 1], (128, 128)
            )
        a = jnp.concatenate([part for part in (new[:at], panel, new[at + 8 :]) if part.shape[0]])
    return a


def inverse_512(a):
    for k in range(4):
        at = slice(128 * k, 128 * k + 128)
        inv = inverse_128(a[k, :, at])
        a[k] = dot(inv, a[k], precision=HIGH)
        a[k, :, at] = inv
        for i in range(4):
            if i != k:
                factor = a[i, :, at]
                a[i, :, at] = jnp.zeros((128, 128), F32)
                a[i] = a[i] - dot(factor, a[k], precision=HIGH)


def tile_of(vec):
    return jnp.concatenate([vec[:, 128 * j : 128 * j + 128] for j in range(4)])


def rows_of(tile):
    vec = jnp.concatenate([tile[2 * j : 2 * j + 2] for j in range(4)], axis=1)
    return jnp.concatenate([vec, jnp.zeros((6, 512), F32)])


def body(
    factor_hbm, couple_hbm, rights_ref, diag_ref, nrhs_ref, link_ref, rdiag_hbm, rrhs_ref,
    leaf_ref, node_ref, root_ref,
    factor, coupling, rdiag, reduced, projected, part, from_core, from_y, from_z, total,
    vec_core, vec_y, vec_z, vec_sum, link, link_t, a, left, e_part, from_x, from_zl, s_all, root, x_rows,
    send, recv, load,
):
    zh, y, core, x, zl = (lax.axis_index(n) for n in AXES)
    scen = zh * 8 + y * 2 + core

    def peer(**at):
        here = dict(zh=zh, y=y, core=core, x=x, zl=zl)
        here.update(at)
        return tuple(here[n] for n in AXES)

    z_peer, core_peer = peer(zh=1 - zh), peer(core=1 - core)
    y_at = [lax.rem(y + d, 4) for d in range(1, 4)]
    x_at = [lax.rem(x + d, 4) for d in range(1, 4)]
    zl_at = [lax.rem(zl + d, 8) for d in range(1, 8)]
    peers = [z_peer, core_peer] + [peer(y=v) for v in y_at] + [peer(x=v) for v in x_at] + [peer(zl=v) for v in zl_at]
    barrier = pltpu.get_barrier_semaphore()
    for device in peers:
        pl.semaphore_signal(barrier, 1, device_id=device, device_id_type=MESH)

    loads = [
        pltpu.make_async_copy(src, dst, load.at[n])
        for n, (src, dst) in enumerate(((couple_hbm, coupling), (factor_hbm, factor), (rdiag_hbm, rdiag)))
    ]
    for copy in loads:
        copy.start()

    used = [0]

    def start(src, dst, device):
        n = used[0]
        used[0] += 1
        copy = pltpu.make_async_remote_copy(
            src_ref=src, dst_ref=dst, send_sem=send.at[n], recv_sem=recv.at[n], device_id=device, device_id_type=MESH
        )
        copy.start()
        return copy

    loads[0].wait()
    loads[1].wait()
    rights = jnp.concatenate([rights_ref[...].astype(F32), jnp.zeros((6, 1024), F32)]).astype(BF16)
    reduced[...] = dot(coupling[...], factor[...], ((0,), (0,))).astype(BF16)
    projected[...] = dot(rights, factor[...])
    for j in range(4):
        part[j, 128 * j :] = dot(reduced[128 * j :], reduced[128 * j : 128 * j + 128], ((1,), (1,)))
    low = projected[...].astype(BF16)
    vec = dot(low, reduced[...], ((1,), (1,)))
    own = pl.ds(pl.multiple_of(32 * scen, 32), 32)
    for j in range(4):
        part[j, own] = part[j, own] + diag_ref[:, 128 * j : 128 * j + 128]
    rows = lax.broadcasted_iota(jnp.int32, (8, 128), 0)
    lanes = lax.broadcasted_iota(jnp.int32, (8, 128), 1)
    strip = jnp.concatenate([nrhs_ref[...]] * 4, axis=1)
    strip = jnp.concatenate([strip] * 4)
    mine = (rows // 2 == scen // 4) & (lanes // 32 == lax.rem(scen, 4))
    vec_core[0] = tile_of(vec[:2]) + jnp.where(mine, strip, 0.0)

    pl.semaphore_wait(barrier, len(peers))

    link[own] = link_ref[...]
    link_far = start(link_ref, link.at[own], z_peer)
    link_near = [start(link_ref, link.at[own], peer(y=v)) for v in y_at]

    half = [256 - 64 * j for j in range(4)]
    piece = [64 - 16 * j for j in range(4)]

    def half_rows(j, c):
        return pl.ds(pl.multiple_of(128 * j + c * half[j], 64), half[j])

    def piece_rows(j, c, v):
        return pl.ds(pl.multiple_of(128 * j + c * half[j] + v * piece[j], 16), piece[j])

    copies = [start(vec_core.at[0], vec_core.at[1], core_peer)]
    for j in range(4):
        copies.append(start(part.at[j, half_rows(j, 1 - core)], from_core.at[j, : half[j]], core_peer))
    for copy in copies:
        copy.wait()
    for j in range(4):
        keep = half_rows(j, core)
        part[j, keep] = part[j, keep] + from_core[j, : half[j]]
    vec_y[y] = vec_core[0] + vec_core[1]

    copies = []
    for d, v in enumerate(y_at):
        copies.append(start(vec_y.at[y], vec_y.at[y], peer(y=v)))
        for j in range(4):
            copies.append(start(part.at[j, piece_rows(j, core, v)], from_y.at[d, j, : piece[j]], peer(y=v)))
    for copy in copies:
        copy.wait()
    for j in range(4):
        from_z[0, j, : piece[j]] = (part[j, piece_rows(j, core, y)] + from_y[0, j, : piece[j]]) + (
            from_y[1, j, : piece[j]] + from_y[2, j, : piece[j]]
        )
    vec_z[0] = (vec_y[0] + vec_y[1]) + (vec_y[2] + vec_y[3])

    copies = [start(vec_z.at[0], vec_z.at[1], z_peer)]
    for j in range(4):
        copies.append(start(from_z.at[0, j, : piece[j]], from_z.at[1, j, : piece[j]], z_peer))
    link_far.wait()
    for copy in link_near:
        copy.wait()
    far = pl.ds(pl.multiple_of(32 * ((1 - zh) * 8 + y * 2 + core), 32), 32)
    link_near = [start(link.at[far], link.at[far], peer(y=v)) for v in y_at]
    for copy in copies:
        copy.wait()
    for j in range(4):
        total[j, piece_rows(j, core, y)] = from_z[0, j, : piece[j]] + from_z[1, j, : piece[j]]
    vec_sum[...] = vec_z[0] + vec_z[1]

    copies = []
    for v in y_at:
        for j in range(4):
            rows_j = piece_rows(j, core, y)
            copies.append(start(total.at[j, rows_j], total.at[j, rows_j], peer(y=v)))
    for copy in copies:
        copy.wait()
    copies = []
    for j in range(4):
        keep = half_rows(j, core)
        copies.append(start(total.at[j, keep], total.at[j, keep], core_peer))
    for copy in link_near:
        copy.wait()
    link_core = []
    for n in range(8):
        at = pl.ds(pl.multiple_of(32 * (2 * n + core), 32), 32)
        link_core.append(start(link.at[at], link.at[at], core_peer))
    for copy in copies:
        copy.wait()

    for j in range(4):
        for i in range(j, 4):
            block = total[j, 128 * i : 128 * i + 128]
            a[i, :, 128 * j : 128 * j + 128] = block
            if i > j:
                a[j, :, 128 * i : 128 * i + 128] = block.T
    inverse_512(a)

    for copy in link_core:
        copy.wait()
    band = pl.ds(pl.multiple_of(128 * y, 128), 128)
    for n in range(4):
        link_t[:, 128 * n : 128 * n + 128] = link[128 * n : 128 * n + 128, band].T
    z_rows = rows_of(vec_sum[...])
    left[:64] = link_t[pl.ds(pl.multiple_of(64 * core, 64), 64)]
    left[64:] = z_rows

    def by_inverse(v):
        out = dot(v[:, :128], a[0], precision=HIGH)
        for n in range(1, 4):
            out = out + dot(v[:, 128 * n : 128 * n + 128], a[n], precision=HIGH)
        return out

    e_rows = dot(by_inverse(left[...]), link[...], precision=HIGH)
    w_tile = tile_of(e_rows[64:66])
    for n in range(4):
        e_part[n, :64] = e_rows[:64, 128 * n : 128 * n + 128]
        e_part[n, 64:] = w_tile

    from_x[x] = e_part[x]
    copies = [start(e_part.at[v], from_x.at[x], peer(x=v)) for v in x_at]
    for copy in copies:
        copy.wait()
    from_zl[zl] = (from_x[0] + from_x[1]) + (from_x[2] + from_x[3])
    copies = [start(from_zl.at[zl], from_zl.at[zl], peer(zl=v)) for v in zl_at]
    for copy in copies:
        copy.wait()
    summed = from_zl[0]
    for n in range(1, 8):
        summed = summed + from_zl[n]
    s_all[core, y, x] = summed[:64]
    w_sum = rows_of(summed[64:])
    copies = [start(s_all.at[core, y, x], s_all.at[core, y, x], peer(x=v)) for v in x_at]
    for copy in copies:
        copy.wait()
    copies = [start(s_all.at[core, y], s_all.at[core, y], peer(y=v)) for v in y_at]
    for copy in copies:
        copy.wait()
    copy = start(s_all.at[core], s_all.at[core], core_peer)
    loads[2].wait()
    copy.wait()
    for i in range(4):
        for c in range(2):
            at = slice(64 * c, 64 * c + 64)
            for n in range(4):
                cols = slice(128 * n, 128 * n + 128)
                root[i, at, cols] = s_all[c, i, n] + rdiag[128 * i + 64 * c : 128 * i + 64 * c + 64, cols]
    inverse_512(root)
    q_rows = jnp.concatenate([rrhs_ref[...], jnp.zeros((6, 512), F32)])
    v = w_sum - q_rows
    root_sol = dot(v[:, :128], root[0], precision=HIGH)
    for n in range(1, 4):
        root_sol = root_sol + dot(v[:, 128 * n : 128 * n + 128], root[n], precision=HIGH)
    root_ref[...] = root_sol[:2]
    shifted = z_rows - dot(root_sol, link[...], ((1,), (1,)), precision=HIGH)
    node_sol = by_inverse(shifted)
    for n in range(16):
        x_rows[n] = node_sol[:2, 32 * n : 32 * n + 32]
    node_ref[...] = x_rows[scen]
    update = dot(node_sol.astype(BF16), reduced[...])
    difference = (update - projected[...]).astype(BF16)
    leaf_ref[...] = dot(difference, factor[...], ((1,), (1,)))[:2]


def local(factors, couple, leaf_rhs, node_diag, node_rhs, link_root, root_diag, root_rhs):
    vmem, hbm = pl.BlockSpec(memory_space=pltpu.VMEM), pl.BlockSpec(memory_space=pl.ANY)
    copies = 80
    leaf, node, root = pl.pallas_call(
        body,
        out_shape=(
            jax.ShapeDtypeStruct((2, 1024), F32),
            jax.ShapeDtypeStruct((2, 32), F32),
            jax.ShapeDtypeStruct((2, 512), F32),
        ),
        in_specs=[hbm, hbm, vmem, vmem, vmem, vmem, hbm, vmem],
        out_specs=(vmem, vmem, vmem),
        scratch_shapes=[
            pltpu.VMEM((1024, 1024), BF16),
            pltpu.VMEM((1024, 512), BF16),
            pltpu.VMEM((512, 512), F32),
            pltpu.VMEM((512, 1024), BF16),
            pltpu.VMEM((8, 1024), F32),
            pltpu.VMEM((4, 512, 128), F32),
            pltpu.VMEM((4, 256, 128), F32),
            pltpu.VMEM((3, 4, 64, 128), F32),
            pltpu.VMEM((2, 4, 64, 128), F32),
            pltpu.VMEM((4, 512, 128), F32),
            pltpu.VMEM((2, 8, 128), F32),
            pltpu.VMEM((4, 8, 128), F32),
            pltpu.VMEM((2, 8, 128), F32),
            pltpu.VMEM((8, 128), F32),
            pltpu.VMEM((512, 512), F32),
            pltpu.VMEM((128, 512), F32),
            pltpu.VMEM((4, 128, 512), F32),
            pltpu.VMEM((72, 512), F32),
            pltpu.VMEM((4, 72, 128), F32),
            pltpu.VMEM((4, 72, 128), F32),
            pltpu.VMEM((8, 72, 128), F32),
            pltpu.VMEM((2, 4, 4, 64, 128), F32),
            pltpu.VMEM((4, 128, 512), F32),
            pltpu.VMEM((16, 2, 32), F32),
            pltpu.SemaphoreType.DMA((copies,)),
            pltpu.SemaphoreType.DMA((copies,)),
            pltpu.SemaphoreType.DMA((3,)),
        ],
        compiler_params=pltpu.CompilerParams(
            collective_id=0, has_side_effects=True, vmem_limit_bytes=48 * 1024 * 1024
        ),
        name="newton",
    )(factors[0, 0], couple[0, 0], leaf_rhs[0, 0], node_diag[0], node_rhs[0], link_root[0], root_diag, root_rhs)
    return (leaf[None, None], node[None], root)


def solution(mesh):
    torus = Mesh(mesh.devices.reshape(2, 4, 2, 4, 8), AXES)
    scen, node = ("zh", "y", "core"), ("x", "zl")
    placed = (
        P(node, scen, None, None),
        P(node, scen, None, None),
        P(node, scen, None, None),
        P(node, scen, None),
        P(node, None, scen),
        P(node, scen, None),
        P(),
        P(),
    )
    return jax.shard_map(
        local,
        mesh=torus,
        in_specs=placed,
        out_specs=(P(node, scen, None, None), P(node, None, scen), P()),
        check_vma=False,
    )
```

```python
import jax
import jax.numpy as jnp
from jax import lax
from jax.experimental import pallas as pl
from jax.experimental.pallas import tpu as pltpu
from jax.sharding import Mesh
from jax.sharding import PartitionSpec as P

AXES = ("zh", "y", "core", "x", "zl")
MESH = pl.DeviceIdType.MESH
HIGH = lax.Precision.HIGHEST
F32 = jnp.float32
BF16 = jnp.bfloat16


def dot(a, b, dims=((1,), (0,)), precision=None):
    return lax.dot_general(a, b, (dims, ((), ())), precision=precision, preferred_element_type=F32)


def reciprocal(x):
    r = pl.reciprocal(x, approx=True)
    h = 1.0 - x * r
    return r + r * (h + h * h)


def inverse_128(a):
    rows = lax.broadcasted_iota(jnp.int32, (8, 128), 0)
    lanes = lax.broadcasted_iota(jnp.int32, (8, 128), 1)
    wide_lanes = lax.broadcasted_iota(jnp.int32, (128, 128), 1)
    for s in range(16):
        at = 8 * s
        panel = a[at : at + 8]
        cols = jnp.stack([jnp.broadcast_to(panel[:, at + j : at + j + 1], (8, 128)) for j in range(8)])
        here = (lanes >= at) & (lanes < at + 8)
        panel = jnp.where(here, jnp.where(lanes - at == rows, 1.0, 0.0), panel)
        for j in range(8):
            mine = rows == j
            col = cols[0]
            inv = reciprocal(jnp.broadcast_to(col[j : j + 1], (8, 128)))
            f = jnp.where(mine, -inv, col * inv)
            if j < 7:
                rest = cols[1:]
                pivot = jnp.broadcast_to(rest[:, j : j + 1], rest.shape)
                cols = jnp.where(mine[None], 0.0, rest) - f[None] * pivot
            panel = jnp.where(mine, 0.0, panel) - f * jnp.broadcast_to(panel[j : j + 1], (8, 128))
        new = jnp.where((wide_lanes >= at) & (wide_lanes < at + 8), 0.0, a)
        for j in range(8):
            new = new - jnp.broadcast_to(a[:, at + j : at + j + 1], (128, 128)) * jnp.broadcast_to(
                panel[j : j + 1], (128, 128)
            )
        a = jnp.concatenate([part for part in (new[:at], panel, new[at + 8 :]) if part.shape[0]])
    return a


def inverse_512(a):
    for k in range(4):
        at = slice(128 * k, 128 * k + 128)
        inv = inverse_128(a[k, :, at])
        a[k] = dot(inv, a[k], precision=HIGH)
        a[k, :, at] = inv
        for i in range(4):
            if i != k:
                factor = a[i, :, at]
                a[i, :, at] = jnp.zeros((128, 128), F32)
                a[i] = a[i] - dot(factor, a[k], precision=HIGH)


def tile_of(vec):
    return jnp.concatenate([vec[:, 128 * j : 128 * j + 128] for j in range(4)])


def rows_of(tile):
    vec = jnp.concatenate([tile[2 * j : 2 * j + 2] for j in range(4)], axis=1)
    return jnp.concatenate([vec, jnp.zeros((6, 512), F32)])


def body(
    factor_hbm, couple_hbm, rights_hbm, diag_hbm, nrhs_hbm, link_hbm, rdiag_hbm, rrhs_hbm,
    leaf_ref, node_ref, root_ref,
    factor, coupling, rights_ref, diag_ref, nrhs_ref, link_ref, rdiag, rrhs_ref, reduced, projected, part, from_core, from_y, from_z, total,
    vec_core, vec_y, vec_z, vec_sum, link, link_t, a, left, e_part, from_x, from_zl, s_all, root, x_rows,
    send, recv, load,
):
    zh, y, core, x, zl = (lax.axis_index(n) for n in AXES)
    scen = zh * 8 + y * 2 + core

    def peer(**at):
        here = dict(zh=zh, y=y, core=core, x=x, zl=zl)
        here.update(at)
        return tuple(here[n] for n in AXES)

    z_peer, core_peer = peer(zh=1 - zh), peer(core=1 - core)
    y_at = [lax.rem(y + d, 4) for d in range(1, 4)]
    x_at = [lax.rem(x + d, 4) for d in range(1, 4)]
    zl_at = [lax.rem(zl + d, 8) for d in range(1, 8)]
    peers = [z_peer, core_peer] + [peer(y=v) for v in y_at] + [peer(x=v) for v in x_at] + [peer(zl=v) for v in zl_at]
    barrier = pltpu.get_barrier_semaphore()
    for device in peers:
        pl.semaphore_signal(barrier, 1, device_id=device, device_id_type=MESH)

    loads = [
        pltpu.make_async_copy(src, dst, load.at[n])
        for n, (src, dst) in enumerate(
            (
                (couple_hbm, coupling),
                (factor_hbm, factor),
                (rights_hbm, rights_ref),
                (diag_hbm, diag_ref),
                (nrhs_hbm, nrhs_ref),
                (link_hbm, link_ref),
                (rdiag_hbm, rdiag),
                (rrhs_hbm, rrhs_ref),
            )
        )
    ]
    for copy in loads:
        copy.start()

    used = [0]

    def start(src, dst, device):
        n = used[0]
        used[0] += 1
        copy = pltpu.make_async_remote_copy(
            src_ref=src, dst_ref=dst, send_sem=send.at[n], recv_sem=recv.at[n], device_id=device, device_id_type=MESH
        )
        copy.start()
        return copy

    for n in range(6):
        loads[n].wait()
    rights = jnp.concatenate([rights_ref[...].astype(F32), jnp.zeros((6, 1024), F32)]).astype(BF16)
    reduced[...] = dot(coupling[...], factor[...], ((0,), (0,))).astype(BF16)
    projected[...] = dot(rights, factor[...])
    for j in range(4):
        part[j, 128 * j :] = dot(reduced[128 * j :], reduced[128 * j : 128 * j + 128], ((1,), (1,)))
    low = projected[...].astype(BF16)
    vec = dot(low, reduced[...], ((1,), (1,)))
    own = pl.ds(pl.multiple_of(32 * scen, 32), 32)
    for j in range(4):
        part[j, own] = part[j, own] + diag_ref[:, 128 * j : 128 * j + 128]
    rows = lax.broadcasted_iota(jnp.int32, (8, 128), 0)
    lanes = lax.broadcasted_iota(jnp.int32, (8, 128), 1)
    strip = jnp.concatenate([nrhs_ref[...]] * 4, axis=1)
    strip = jnp.concatenate([strip] * 4)
    mine = (rows // 2 == scen // 4) & (lanes // 32 == lax.rem(scen, 4))
    vec_core[0] = tile_of(vec[:2]) + jnp.where(mine, strip, 0.0)

    pl.semaphore_wait(barrier, len(peers))

    link[own] = link_ref[...]
    link_far = start(link_ref, link.at[own], z_peer)
    link_near = [start(link_ref, link.at[own], peer(y=v)) for v in y_at]

    half = [256 - 64 * j for j in range(4)]
    piece = [64 - 16 * j for j in range(4)]

    def half_rows(j, c):
        return pl.ds(pl.multiple_of(128 * j + c * half[j], 64), half[j])

    def piece_rows(j, c, v):
        return pl.ds(pl.multiple_of(128 * j + c * half[j] + v * piece[j], 16), piece[j])

    copies = [start(vec_core.at[0], vec_core.at[1], core_peer)]
    for j in range(4):
        copies.append(start(part.at[j, half_rows(j, 1 - core)], from_core.at[j, : half[j]], core_peer))
    for copy in copies:
        copy.wait()
    for j in range(4):
        keep = half_rows(j, core)
        part[j, keep] = part[j, keep] + from_core[j, : half[j]]
    vec_y[y] = vec_core[0] + vec_core[1]

    copies = []
    for d, v in enumerate(y_at):
        copies.append(start(vec_y.at[y], vec_y.at[y], peer(y=v)))
        for j in range(4):
            copies.append(start(part.at[j, piece_rows(j, core, v)], from_y.at[d, j, : piece[j]], peer(y=v)))
    for copy in copies:
        copy.wait()
    for j in range(4):
        from_z[0, j, : piece[j]] = (part[j, piece_rows(j, core, y)] + from_y[0, j, : piece[j]]) + (
            from_y[1, j, : piece[j]] + from_y[2, j, : piece[j]]
        )
    vec_z[0] = (vec_y[0] + vec_y[1]) + (vec_y[2] + vec_y[3])

    copies = [start(vec_z.at[0], vec_z.at[1], z_peer)]
    for j in range(4):
        copies.append(start(from_z.at[0, j, : piece[j]], from_z.at[1, j, : piece[j]], z_peer))
    link_far.wait()
    for copy in link_near:
        copy.wait()
    far = pl.ds(pl.multiple_of(32 * ((1 - zh) * 8 + y * 2 + core), 32), 32)
    link_near = [start(link.at[far], link.at[far], peer(y=v)) for v in y_at]
    for copy in copies:
        copy.wait()
    for j in range(4):
        total[j, piece_rows(j, core, y)] = from_z[0, j, : piece[j]] + from_z[1, j, : piece[j]]
    vec_sum[...] = vec_z[0] + vec_z[1]

    copies = []
    for v in y_at:
        for j in range(4):
            rows_j = piece_rows(j, core, y)
            copies.append(start(total.at[j, rows_j], total.at[j, rows_j], peer(y=v)))
    for copy in copies:
        copy.wait()
    copies = []
    for j in range(4):
        keep = half_rows(j, core)
        copies.append(start(total.at[j, keep], total.at[j, keep], core_peer))
    for copy in link_near:
        copy.wait()
    link_core = []
    for n in range(8):
        at = pl.ds(pl.multiple_of(32 * (2 * n + core), 32), 32)
        link_core.append(start(link.at[at], link.at[at], core_peer))
    for copy in copies:
        copy.wait()

    for j in range(4):
        for i in range(j, 4):
            block = total[j, 128 * i : 128 * i + 128]
            a[i, :, 128 * j : 128 * j + 128] = block
            if i > j:
                a[j, :, 128 * i : 128 * i + 128] = block.T
    inverse_512(a)

    for copy in link_core:
        copy.wait()
    band = pl.ds(pl.multiple_of(128 * y, 128), 128)
    for n in range(4):
        link_t[:, 128 * n : 128 * n + 128] = link[128 * n : 128 * n + 128, band].T
    z_rows = rows_of(vec_sum[...])
    left[:64] = link_t[pl.ds(pl.multiple_of(64 * core, 64), 64)]
    left[64:] = z_rows

    def by_inverse(v):
        out = dot(v[:, :128], a[0], precision=HIGH)
        for n in range(1, 4):
            out = out + dot(v[:, 128 * n : 128 * n + 128], a[n], precision=HIGH)
        return out

    e_rows = dot(by_inverse(left[...]), link[...], precision=HIGH)
    w_tile = tile_of(e_rows[64:66])
    for n in range(4):
        e_part[n, :64] = e_rows[:64, 128 * n : 128 * n + 128]
        e_part[n, 64:] = w_tile

    from_x[x] = e_part[x]
    copies = [start(e_part.at[v], from_x.at[x], peer(x=v)) for v in x_at]
    for copy in copies:
        copy.wait()
    from_zl[zl] = (from_x[0] + from_x[1]) + (from_x[2] + from_x[3])
    copies = [start(from_zl.at[zl], from_zl.at[zl], peer(zl=v)) for v in zl_at]
    for copy in copies:
        copy.wait()
    summed = from_zl[0]
    for n in range(1, 8):
        summed = summed + from_zl[n]
    s_all[core, y, x] = summed[:64]
    w_sum = rows_of(summed[64:])
    copies = [start(s_all.at[core, y, x], s_all.at[core, y, x], peer(x=v)) for v in x_at]
    for copy in copies:
        copy.wait()
    copies = [start(s_all.at[core, y], s_all.at[core, y], peer(y=v)) for v in y_at]
    for copy in copies:
        copy.wait()
    copy = start(s_all.at[core], s_all.at[core], core_peer)
    loads[6].wait()
    loads[7].wait()
    copy.wait()
    for i in range(4):
        for c in range(2):
            at = slice(64 * c, 64 * c + 64)
            for n in range(4):
                cols = slice(128 * n, 128 * n + 128)
                root[i, at, cols] = s_all[c, i, n] + rdiag[128 * i + 64 * c : 128 * i + 64 * c + 64, cols]
    inverse_512(root)
    q_rows = jnp.concatenate([rrhs_ref[...], jnp.zeros((6, 512), F32)])
    v = w_sum - q_rows
    root_sol = dot(v[:, :128], root[0], precision=HIGH)
    for n in range(1, 4):
        root_sol = root_sol + dot(v[:, 128 * n : 128 * n + 128], root[n], precision=HIGH)
    root_ref[...] = root_sol[:2]
    shifted = z_rows - dot(root_sol, link[...], ((1,), (1,)), precision=HIGH)
    node_sol = by_inverse(shifted)
    for n in range(16):
        x_rows[n] = node_sol[:2, 32 * n : 32 * n + 32]
    node_ref[...] = x_rows[scen]
    update = dot(node_sol.astype(BF16), reduced[...])
    difference = (update - projected[...]).astype(BF16)
    leaf_ref[...] = dot(difference, factor[...], ((1,), (1,)))[:2]


def local(factors, couple, leaf_rhs, node_diag, node_rhs, link_root, root_diag, root_rhs):
    vmem, hbm = pl.BlockSpec(memory_space=pltpu.VMEM), pl.BlockSpec(memory_space=pl.ANY)
    copies = 80
    leaf, node, root = pl.pallas_call(
        body,
        out_shape=(
            jax.ShapeDtypeStruct((2, 1024), F32),
            jax.ShapeDtypeStruct((2, 32), F32),
            jax.ShapeDtypeStruct((2, 512), F32),
        ),
        in_specs=[hbm] * 8,
        out_specs=(vmem, vmem, vmem),
        scratch_shapes=[
            pltpu.VMEM((1024, 1024), BF16),
            pltpu.VMEM((1024, 512), BF16),
            pltpu.VMEM((2, 1024), BF16),
            pltpu.VMEM((32, 512), F32),
            pltpu.VMEM((2, 32), F32),
            pltpu.VMEM((32, 512), F32),
            pltpu.VMEM((512, 512), F32),
            pltpu.VMEM((2, 512), F32),
            pltpu.VMEM((512, 1024), BF16),
            pltpu.VMEM((8, 1024), F32),
            pltpu.VMEM((4, 512, 128), F32),
            pltpu.VMEM((4, 256, 128), F32),
            pltpu.VMEM((3, 4, 64, 128), F32),
            pltpu.VMEM((2, 4, 64, 128), F32),
            pltpu.VMEM((4, 512, 128), F32),
            pltpu.VMEM((2, 8, 128), F32),
            pltpu.VMEM((4, 8, 128), F32),
            pltpu.VMEM((2, 8, 128), F32),
            pltpu.VMEM((8, 128), F32),
            pltpu.VMEM((512, 512), F32),
            pltpu.VMEM((128, 512), F32),
            pltpu.VMEM((4, 128, 512), F32),
            pltpu.VMEM((72, 512), F32),
            pltpu.VMEM((4, 72, 128), F32),
            pltpu.VMEM((4, 72, 128), F32),
            pltpu.VMEM((8, 72, 128), F32),
            pltpu.VMEM((2, 4, 4, 64, 128), F32),
            pltpu.VMEM((4, 128, 512), F32),
            pltpu.VMEM((16, 2, 32), F32),
            pltpu.SemaphoreType.DMA((copies,)),
            pltpu.SemaphoreType.DMA((copies,)),
            pltpu.SemaphoreType.DMA((8,)),
        ],
        compiler_params=pltpu.CompilerParams(
            collective_id=0, has_side_effects=True, vmem_limit_bytes=60 * 1024 * 1024
        ),
        name="newton",
    )(factors[0, 0], couple[0, 0], leaf_rhs[0, 0], node_diag[0], node_rhs[0], link_root[0], root_diag, root_rhs)
    return (leaf[None, None], node[None], root)


def solution(mesh):
    torus = Mesh(mesh.devices.reshape(2, 4, 2, 4, 8), AXES)
    scen, node = ("zh", "y", "core"), ("x", "zl")
    placed = (
        P(node, scen, None, None),
        P(node, scen, None, None),
        P(node, scen, None, None),
        P(node, scen, None),
        P(node, None, scen),
        P(node, scen, None),
        P(),
        P(),
    )
    return jax.shard_map(
        local,
        mesh=torus,
        in_specs=placed,
        out_specs=(P(node, scen, None, None), P(node, None, scen), P()),
        check_vma=False,
    )
```

```python
import jax
import jax.numpy as jnp
from jax import lax
from jax.experimental import pallas as pl
from jax.experimental.pallas import tpu as pltpu
from jax.sharding import Mesh
from jax.sharding import PartitionSpec as P

AXES = ("zh", "y", "core", "x", "zl")
MESH = pl.DeviceIdType.MESH
HIGH = lax.Precision.HIGHEST
F32 = jnp.float32
BF16 = jnp.bfloat16


def dot(a, b, dims=((1,), (0,)), precision=None):
    return lax.dot_general(a, b, (dims, ((), ())), precision=precision, preferred_element_type=F32)


def inverse_128(a, work=()):
    rows = lax.broadcasted_iota(jnp.int32, (8, 128), 0)
    lanes = lax.broadcasted_iota(jnp.int32, (8, 128), 1)
    wide_lanes = lax.broadcasted_iota(jnp.int32, (128, 128), 1)
    work = list(work)
    for s in range(16):
        at = 8 * s
        panel = a[at : at + 8]
        cols = jnp.stack([jnp.broadcast_to(panel[:, at + j : at + j + 1], (8, 128)) for j in range(8)])
        here = (lanes >= at) & (lanes < at + 8)
        panel = jnp.where(here, jnp.where(lanes - at == rows, 1.0, 0.0), panel)
        for j in range(8):
            mine = rows == j
            col = cols[0]
            inv = pl.reciprocal(jnp.broadcast_to(col[j : j + 1], (8, 128)), approx=True)
            f = jnp.where(mine, -inv, col * inv)
            if j < 7:
                rest = cols[1:]
                pivot = jnp.broadcast_to(rest[:, j : j + 1], rest.shape)
                cols = jnp.where(mine[None], 0.0, rest) - f[None] * pivot
            panel = jnp.where(mine, 0.0, panel) - f * jnp.broadcast_to(panel[j : j + 1], (8, 128))
        new = jnp.where((wide_lanes >= at) & (wide_lanes < at + 8), 0.0, a)
        for j in range(8):
            new = new - jnp.broadcast_to(a[:, at + j : at + j + 1], (128, 128)) * jnp.broadcast_to(
                panel[j : j + 1], (128, 128)
            )
        a = jnp.concatenate([part for part in (new[:at], panel, new[at + 8 :]) if part.shape[0]])
        left = 16 - s
        for _ in range(-(-len(work) // left)):
            work.pop(0)()
    for w in work:
        w()
    return a
def inverse_512(a, between=None):
    work = []
    cols = [slice(128 * n, 128 * n + 128) for n in range(4)]
    for k in range(4):
        inv = inverse_128(a[k, :, cols[k]], work)
        if between is not None:
            between(k)
        work = []
        nxt = k + 1
        def row(j, k=k, inv=inv):
            a[k, :, cols[j]] = dot(inv, a[k, :, cols[j]], precision=HIGH)
        def update(i, j, k=k):
            a[i, :, cols[j]] = a[i, :, cols[j]] - dot(a[i, :, cols[k]], a[k, :, cols[j]], precision=HIGH)
        def column(i, k=k, inv=inv):
            a[i, :, cols[k]] = -dot(a[i, :, cols[k]], inv, precision=HIGH)
        others = [n for n in range(4) if n != k]
        if nxt < 4:
            row(nxt); update(nxt, nxt)
        for j in others:
            if j != nxt: work.append(lambda j=j, f=row: f(j))
        for j in others:
            for i in others:
                if not (i == j == nxt): work.append(lambda i=i, j=j, f=update: f(i, j))
        for i in others: work.append(lambda i=i, f=column: f(i))
        def keep(k=k, inv=inv):
            a[k, :, cols[k]] = inv

        work.append(keep)
    for w in work:
        w()


def tile_of(vec):
    return jnp.concatenate([vec[:, 128 * j : 128 * j + 128] for j in range(4)])


def rows_of(tile):
    vec = jnp.concatenate([tile[2 * j : 2 * j + 2] for j in range(4)], axis=1)
    return jnp.concatenate([vec, jnp.zeros((6, 512), F32)])


def body(
    factor_hbm, couple_hbm, rights_hbm, diag_hbm, nrhs_hbm, link_hbm, rdiag_hbm, rrhs_hbm,
    leaf_ref, node_ref, root_ref,
    factor, coupling, rights_ref, diag_ref, nrhs_ref, link_ref, rdiag, rrhs_ref, reduced, projected, part, first, first_from, first_z, first_sum,
    rest, rest_from, rest_z, rest_sum, link, link_t, a, left, e_part, from_x, from_zl, s_all, root, x_rows,
    send, recv, load,
):
    zh, y, core, x, zl = (lax.axis_index(n) for n in AXES)
    scen = zh * 8 + y * 2 + core

    def peer(**at):
        here = dict(zh=zh, y=y, core=core, x=x, zl=zl)
        here.update(at)
        return tuple(here[n] for n in AXES)

    z_peer, core_peer = peer(zh=1 - zh), peer(core=1 - core)
    y_at = [lax.rem(y + d, 4) for d in range(1, 4)]
    x_at = [lax.rem(x + d, 4) for d in range(1, 4)]
    zl_at = [lax.rem(zl + d, 8) for d in range(1, 8)]
    peers = [z_peer, core_peer] + [peer(y=v) for v in y_at] + [peer(x=v) for v in x_at] + [peer(zl=v) for v in zl_at]
    barrier = pltpu.get_barrier_semaphore()
    for device in peers:
        pl.semaphore_signal(barrier, 1, device_id=device, device_id_type=MESH)

    loads = [
        pltpu.make_async_copy(src, dst, load.at[n])
        for n, (src, dst) in enumerate(
            (
                (couple_hbm, coupling),
                (factor_hbm, factor),
                (rights_hbm, rights_ref),
                (diag_hbm, diag_ref),
                (nrhs_hbm, nrhs_ref),
                (link_hbm, link_ref),
                (rdiag_hbm, rdiag),
                (rrhs_hbm, rrhs_ref),
            )
        )
    ]
    for copy in loads:
        copy.start()

    used = [0]

    def start(src, dst, device):
        n = used[0]
        used[0] += 1
        copy = pltpu.make_async_remote_copy(
            src_ref=src, dst_ref=dst, send_sem=send.at[n], recv_sem=recv.at[n], device_id=device, device_id_type=MESH
        )
        copy.start()
        return copy

    for n in range(6):
        loads[n].wait()
    rights = jnp.concatenate([rights_ref[...].astype(F32), jnp.zeros((6, 1024), F32)]).astype(BF16)
    reduced[...] = dot(coupling[...], factor[...], ((0,), (0,))).astype(BF16)
    projected[...] = dot(rights, factor[...])
    for j in range(4):
        part[j, 128 * j :] = dot(reduced[128 * j :], reduced[128 * j : 128 * j + 128], ((1,), (1,)))
    low = projected[...].astype(BF16)
    vec = dot(low, reduced[...], ((1,), (1,)))
    own = pl.ds(pl.multiple_of(32 * scen, 32), 32)
    for j in range(4):
        part[j, own] = part[j, own] + diag_ref[:, 128 * j : 128 * j + 128]
    rows = lax.broadcasted_iota(jnp.int32, (8, 128), 0)
    lanes = lax.broadcasted_iota(jnp.int32, (8, 128), 1)
    strip = jnp.concatenate([nrhs_ref[...]] * 4, axis=1)
    strip = jnp.concatenate([strip] * 4)
    mine = (rows // 2 == scen // 4) & (lanes // 32 == lax.rem(scen, 4))
    vec_tile = tile_of(vec[:2]) + jnp.where(mine, strip, 0.0)
    for c in range(2):
        for v in range(4):
            p = 4 * c + v
            first[c, v] = part[0, 16 * p : 16 * p + 16]
            rest[c, v, 0:48] = part[0, 128 + 48 * p : 176 + 48 * p]
            rest[c, v, 48:96] = part[1, 128 + 48 * p : 176 + 48 * p]
            rest[c, v, 96:128] = part[2, 256 + 32 * p : 288 + 32 * p]
            rest[c, v, 128:144] = part[3, 384 + 16 * p : 400 + 16 * p]
            rest[c, v, 144:152] = vec_tile

    pl.semaphore_wait(barrier, len(peers))

    first_core = start(first.at[1 - core], first_from.at[0], core_peer)
    rest_core = start(rest.at[1 - core], rest_from.at[0], core_peer)
    first_core.wait()
    first[core] = first[core] + first_from[0]
    first_y = [start(first.at[core, v], first_from.at[1, d], peer(y=v)) for d, v in enumerate(y_at)]
    rest_core.wait()
    rest[core] = rest[core] + rest_from[0]
    rest_y = [start(rest.at[core, v], rest_from.at[1, d], peer(y=v)) for d, v in enumerate(y_at)]
    for copy in first_y:
        copy.wait()
    first_z[0] = (first[core, y] + first_from[1, 0]) + (first_from[1, 1] + first_from[1, 2])
    first_far = start(first_z.at[0], first_z.at[1], z_peer)
    for copy in rest_y:
        copy.wait()
    rest_z[0] = (rest[core, y] + rest_from[1, 0]) + (rest_from[1, 1] + rest_from[1, 2])
    rest_far = start(rest_z.at[0], rest_z.at[1], z_peer)

    first_far.wait()
    first_sum[core, y] = first_z[0] + first_z[1]
    first_y = [start(first_sum.at[core, y], first_sum.at[core, y], peer(y=v)) for v in y_at]
    rest_far.wait()
    rest_sum[core, y] = rest_z[0] + rest_z[1]
    rest_y = [start(rest_sum.at[core, y], rest_sum.at[core, y], peer(y=v)) for v in y_at]
    for copy in first_y:
        copy.wait()
    first_core = start(first_sum.at[core], first_sum.at[core], core_peer)
    for copy in rest_y:
        copy.wait()
    rest_core = start(rest_sum.at[core], rest_sum.at[core], core_peer)
    link[own] = link_ref[...]
    link_far = start(link_ref, link.at[own], z_peer)
    link_near = [start(link_ref, link.at[own], peer(y=v)) for v in y_at]
    first_core.wait()
    a[0, :, :128] = jnp.concatenate([first_sum[p // 4, p % 4] for p in range(8)])
    later = {}

    def between(k):
        if k == 0:
            rest_core.wait()
            spans = ((0, 1, 0, 48), (1, 1, 48, 48), (2, 2, 96, 32), (3, 3, 128, 16))
            for j, i0, low_row, n in spans:
                column = jnp.concatenate([rest_sum[p // 4, p % 4, low_row : low_row + n] for p in range(8)])
                for i in range(i0, 4):
                    block = column[128 * (i - i0) : 128 * (i - i0) + 128]
                    a[i, :, 128 * j : 128 * j + 128] = block
                    if i > j:
                        a[j, :, 128 * i : 128 * i + 128] = block.T
        if k == 1:
            link_far.wait()
            for copy in link_near:
                copy.wait()
            far = pl.ds(pl.multiple_of(32 * ((1 - zh) * 8 + y * 2 + core), 32), 32)
            later["near"] = [start(link.at[far], link.at[far], peer(y=v)) for v in y_at]
        if k == 2:
            for copy in later["near"]:
                copy.wait()
            later["core"] = []
            for n in range(8):
                at = pl.ds(pl.multiple_of(32 * (2 * n + core), 32), 32)
                later["core"].append(start(link.at[at], link.at[at], core_peer))

    inverse_512(a, between)
    for copy in later["core"]:
        copy.wait()
    vec_total = rest_sum[core, y, 144:]

    band = pl.ds(pl.multiple_of(128 * y, 128), 128)
    for n in range(4):
        link_t[:, 128 * n : 128 * n + 128] = link[128 * n : 128 * n + 128, band].T
    z_rows = rows_of(vec_total)
    left[:64] = link_t[pl.ds(pl.multiple_of(64 * core, 64), 64)]
    left[64:] = z_rows

    def by_inverse(v):
        out = dot(v[:, :128], a[0], precision=HIGH)
        for n in range(1, 4):
            out = out + dot(v[:, 128 * n : 128 * n + 128], a[n], precision=HIGH)
        return out

    e_rows = dot(by_inverse(left[...]), link[...], precision=HIGH)
    w_tile = tile_of(e_rows[64:66])
    for n in range(4):
        e_part[n, :64] = e_rows[:64, 128 * n : 128 * n + 128]
        e_part[n, 64:] = w_tile

    from_x[x] = e_part[x]
    copies = [start(e_part.at[v], from_x.at[x], peer(x=v)) for v in x_at]
    for copy in copies:
        copy.wait()
    from_zl[zl] = (from_x[0] + from_x[1]) + (from_x[2] + from_x[3])
    copies = [start(from_zl.at[zl], from_zl.at[zl], peer(zl=v)) for v in zl_at]
    for copy in copies:
        copy.wait()
    summed = from_zl[0]
    for n in range(1, 8):
        summed = summed + from_zl[n]
    s_all[core, y, x] = summed[:64]
    w_sum = rows_of(summed[64:])
    copies = [start(s_all.at[core, y, x], s_all.at[core, y, x], peer(x=v)) for v in x_at]
    for copy in copies:
        copy.wait()
    copies = [start(s_all.at[core, y], s_all.at[core, y], peer(y=v)) for v in y_at]
    for copy in copies:
        copy.wait()
    copy = start(s_all.at[core], s_all.at[core], core_peer)
    loads[6].wait()
    loads[7].wait()
    copy.wait()
    for i in range(4):
        for c in range(2):
            at = slice(64 * c, 64 * c + 64)
            for n in range(4):
                cols = slice(128 * n, 128 * n + 128)
                root[i, at, cols] = s_all[c, i, n] + rdiag[128 * i + 64 * c : 128 * i + 64 * c + 64, cols]
    inverse_512(root)
    q_rows = jnp.concatenate([rrhs_ref[...], jnp.zeros((6, 512), F32)])
    v = w_sum - q_rows
    root_sol = dot(v[:, :128], root[0], precision=HIGH)
    for n in range(1, 4):
        root_sol = root_sol + dot(v[:, 128 * n : 128 * n + 128], root[n], precision=HIGH)
    root_ref[...] = root_sol[:2]
    shifted = z_rows - dot(root_sol, link[...], ((1,), (1,)), precision=HIGH)
    node_sol = by_inverse(shifted)
    for n in range(16):
        x_rows[n] = node_sol[:2, 32 * n : 32 * n + 32]
    node_ref[...] = x_rows[scen]
    update = dot(node_sol.astype(BF16), reduced[...])
    difference = (update - projected[...]).astype(BF16)
    leaf_ref[...] = dot(difference, factor[...], ((1,), (1,)))[:2]


def local(factors, couple, leaf_rhs, node_diag, node_rhs, link_root, root_diag, root_rhs):
    vmem, hbm = pl.BlockSpec(memory_space=pltpu.VMEM), pl.BlockSpec(memory_space=pl.ANY)
    copies = 64
    leaf, node, root = pl.pallas_call(
        body,
        out_shape=(
            jax.ShapeDtypeStruct((2, 1024), F32),
            jax.ShapeDtypeStruct((2, 32), F32),
            jax.ShapeDtypeStruct((2, 512), F32),
        ),
        in_specs=[hbm] * 8,
        out_specs=(vmem, vmem, vmem),
        scratch_shapes=[
            pltpu.VMEM((1024, 1024), BF16),
            pltpu.VMEM((1024, 512), BF16),
            pltpu.VMEM((2, 1024), BF16),
            pltpu.VMEM((32, 512), F32),
            pltpu.VMEM((2, 32), F32),
            pltpu.VMEM((32, 512), F32),
            pltpu.VMEM((512, 512), F32),
            pltpu.VMEM((2, 512), F32),
            pltpu.VMEM((512, 1024), BF16),
            pltpu.VMEM((8, 1024), F32),
            pltpu.VMEM((4, 512, 128), F32),
            pltpu.VMEM((2, 4, 16, 128), F32),
            pltpu.VMEM((2, 4, 16, 128), F32),
            pltpu.VMEM((2, 16, 128), F32),
            pltpu.VMEM((2, 4, 16, 128), F32),
            pltpu.VMEM((2, 4, 152, 128), F32),
            pltpu.VMEM((2, 4, 152, 128), F32),
            pltpu.VMEM((2, 152, 128), F32),
            pltpu.VMEM((2, 4, 152, 128), F32),
            pltpu.VMEM((512, 512), F32),
            pltpu.VMEM((128, 512), F32),
            pltpu.VMEM((4, 128, 512), F32),
            pltpu.VMEM((72, 512), F32),
            pltpu.VMEM((4, 72, 128), F32),
            pltpu.VMEM((4, 72, 128), F32),
            pltpu.VMEM((8, 72, 128), F32),
            pltpu.VMEM((2, 4, 4, 64, 128), F32),
            pltpu.VMEM((4, 128, 512), F32),
            pltpu.VMEM((16, 2, 32), F32),
            pltpu.SemaphoreType.DMA((copies,)),
            pltpu.SemaphoreType.DMA((copies,)),
            pltpu.SemaphoreType.DMA((8,)),
        ],
        compiler_params=pltpu.CompilerParams(
            collective_id=0, has_side_effects=True, vmem_limit_bytes=60 * 1024 * 1024
        ),
        name="newton",
    )(factors[0, 0], couple[0, 0], leaf_rhs[0, 0], node_diag[0], node_rhs[0], link_root[0], root_diag, root_rhs)
    return (leaf[None, None], node[None], root)


def solution(mesh):
    torus = Mesh(mesh.devices.reshape(2, 4, 2, 4, 8), AXES)
    scen, node = ("zh", "y", "core"), ("x", "zl")
    placed = (
        P(node, scen, None, None),
        P(node, scen, None, None),
        P(node, scen, None, None),
        P(node, scen, None),
        P(node, None, scen),
        P(node, scen, None),
        P(),
        P(),
    )
    return jax.shard_map(
        local,
        mesh=torus,
        in_specs=placed,
        out_specs=(P(node, scen, None, None), P(node, None, scen), P()),
        check_vma=False,
    )
```

```python
import jax
import jax.numpy as jnp
from jax import lax
from jax.experimental import pallas as pl
from jax.experimental.pallas import tpu as pltpu
from jax.sharding import Mesh
from jax.sharding import PartitionSpec as P

AXES = ("zh", "y", "core", "x", "zl")
MESH = pl.DeviceIdType.MESH
HIGH = lax.Precision.HIGHEST
F32 = jnp.float32
BF16 = jnp.bfloat16


def dot(a, b, dims=((1,), (0,)), precision=None):
    return lax.dot_general(a, b, (dims, ((), ())), precision=precision, preferred_element_type=F32)


def thirds(v):
    high = v.astype(BF16).astype(F32)
    mid = (v - high).astype(BF16).astype(F32)
    return high, mid, v - high - mid


def inverse_128(a, work=()):
    rows = lax.broadcasted_iota(jnp.int32, (8, 128), 0)
    lanes = lax.broadcasted_iota(jnp.int32, (8, 128), 1)
    wide_lanes = lax.broadcasted_iota(jnp.int32, (128, 128), 1)
    work = list(work)
    following = a[:8]
    for s in range(16):
        at = 8 * s
        panel = following
        ah, am, al = thirds(jnp.where(lanes < at, -panel, panel))
        cols = jnp.stack([jnp.broadcast_to(panel[:, at + j : at + j + 1], (8, 128)) for j in range(8)])
        here = (lanes >= at) & (lanes < at + 8)
        panel = jnp.where(here, jnp.where(lanes - at == rows, 1.0, 0.0), panel)
        for j in range(8):
            mine = rows == j
            col = cols[0]
            inv = pl.reciprocal(jnp.broadcast_to(col[j : j + 1], (8, 128)), approx=True)
            f = jnp.where(mine, -inv, col * inv)
            if j < 7:
                rest = cols[1:]
                pivot = jnp.broadcast_to(rest[:, j : j + 1], rest.shape)
                cols = jnp.where(mine[None], 0.0, rest) - f[None] * pivot
            panel = jnp.where(mine, 0.0, panel) - f * jnp.broadcast_to(panel[j : j + 1], (8, 128))
        if s < 15:
            old = a[at + 8 : at + 16]
            following = jnp.where(here, 0.0, old)
            for j in range(8):
                following = following - jnp.broadcast_to(old[:, at + j : at + j + 1], (8, 128)) * jnp.broadcast_to(
                    panel[j : j + 1], (8, 128)
                )
        bh, bm, bl = thirds(panel)
        left = jnp.concatenate([ah, ah, ah, am, am, al]).astype(BF16)
        right = jnp.concatenate([bh, bm, bl, bh, bm, bh]).astype(BF16)
        new = jnp.where((wide_lanes >= at) & (wide_lanes < at + 8), 0.0, a) - dot(left, right, ((0,), (0,)))
        a = jnp.concatenate([part for part in (new[:at], panel, new[at + 8 :]) if part.shape[0]])
        for _ in range(-(-len(work) // (16 - s))):
            work.pop(0)()
    return a


def inverse_512(a, between=None):
    work = []
    cols = [slice(128 * n, 128 * n + 128) for n in range(4)]
    for k in range(4):
        inv = inverse_128(a[k, :, cols[k]], work)
        if between is not None:
            between(k)
        work = []
        nxt = k + 1
        def row(j, k=k, inv=inv):
            a[k, :, cols[j]] = dot(inv, a[k, :, cols[j]], precision=HIGH)
        def update(i, j, k=k):
            a[i, :, cols[j]] = a[i, :, cols[j]] - dot(a[i, :, cols[k]], a[k, :, cols[j]], precision=HIGH)
        def column(i, k=k, inv=inv):
            a[i, :, cols[k]] = -dot(a[i, :, cols[k]], inv, precision=HIGH)
        others = [n for n in range(4) if n != k]
        if nxt < 4:
            row(nxt); update(nxt, nxt)
        for j in others:
            if j != nxt: work.append(lambda j=j, f=row: f(j))
        for j in others:
            for i in others:
                if not (i == j == nxt): work.append(lambda i=i, j=j, f=update: f(i, j))
        for i in others: work.append(lambda i=i, f=column: f(i))
        def keep(k=k, inv=inv):
            a[k, :, cols[k]] = inv

        work.append(keep)
    for w in work:
        w()


def tile_of(vec):
    return jnp.concatenate([vec[:, 128 * j : 128 * j + 128] for j in range(4)])


def rows_of(tile):
    vec = jnp.concatenate([tile[2 * j : 2 * j + 2] for j in range(4)], axis=1)
    return jnp.concatenate([vec, jnp.zeros((6, 512), F32)])


def body(
    factor_hbm, couple_hbm, rights_hbm, diag_hbm, nrhs_hbm, link_hbm, rdiag_hbm, rrhs_hbm,
    out_ref,
    factor, coupling, rights_ref, diag_ref, nrhs_ref, link_ref, rdiag, rrhs_ref, reduced, projected, part, first, first_from, first_z, first_sum,
    rest, rest_from, rest_z, rest_sum, link, link_t, a, left, e_part, from_x, from_zl, back, s_all, root, x_rows,
    send, recv, load,
):
    zh, y, core, x, zl = (lax.axis_index(n) for n in AXES)
    scen = zh * 8 + y * 2 + core

    def peer(**at):
        here = dict(zh=zh, y=y, core=core, x=x, zl=zl)
        here.update(at)
        return tuple(here[n] for n in AXES)

    z_peer, core_peer = peer(zh=1 - zh), peer(core=1 - core)
    y_at = [lax.rem(y + d, 4) for d in range(1, 4)]
    x_at = [lax.rem(x + d, 4) for d in range(1, 4)]
    zl_at = [lax.rem(zl + d, 8) for d in range(1, 8)]
    peers = [z_peer, core_peer] + [peer(y=v) for v in y_at] + [peer(x=v) for v in x_at] + [peer(zl=v) for v in zl_at]
    barrier = pltpu.get_barrier_semaphore()
    for device in peers:
        pl.semaphore_signal(barrier, 1, device_id=device, device_id_type=MESH)

    loads = [
        pltpu.make_async_copy(src, dst, load.at[n])
        for n, (src, dst) in enumerate(
            (
                (couple_hbm, coupling),
                (factor_hbm, factor),
                (rights_hbm, rights_ref),
                (diag_hbm, diag_ref),
                (nrhs_hbm, nrhs_ref),
                (link_hbm, link_ref),
                (rdiag_hbm, rdiag),
                (rrhs_hbm, rrhs_ref),
            )
        )
    ]
    for copy in loads:
        copy.start()

    used = [0]

    def start(src, dst, device):
        n = used[0]
        used[0] += 1
        copy = pltpu.make_async_remote_copy(
            src_ref=src, dst_ref=dst, send_sem=send.at[n], recv_sem=recv.at[n], device_id=device, device_id_type=MESH
        )
        copy.start()
        return copy

    for n in range(6):
        loads[n].wait()
    rights = jnp.concatenate([rights_ref[...].astype(F32), jnp.zeros((6, 1024), F32)]).astype(BF16)
    reduced[...] = dot(coupling[...], factor[...], ((0,), (0,))).astype(BF16)
    projected[...] = dot(rights, factor[...])
    for j in range(4):
        part[j, 128 * j :] = dot(reduced[128 * j :], reduced[128 * j : 128 * j + 128], ((1,), (1,)))
    low = projected[...].astype(BF16)
    vec = dot(low, reduced[...], ((1,), (1,)))
    own = pl.ds(pl.multiple_of(32 * scen, 32), 32)
    for j in range(4):
        part[j, own] = part[j, own] + diag_ref[:, 128 * j : 128 * j + 128]
    rows = lax.broadcasted_iota(jnp.int32, (8, 128), 0)
    lanes = lax.broadcasted_iota(jnp.int32, (8, 128), 1)
    strip = jnp.concatenate([nrhs_ref[...]] * 4, axis=1)
    strip = jnp.concatenate([strip] * 4)
    mine = (rows // 2 == scen // 4) & (lanes // 32 == lax.rem(scen, 4))
    vec_tile = tile_of(vec[:2]) + jnp.where(mine, strip, 0.0)
    for c in range(2):
        for v in range(4):
            p = 4 * c + v
            first[c, v] = part[0, 16 * p : 16 * p + 16]
            rest[c, v, 0:48] = part[0, 128 + 48 * p : 176 + 48 * p]
            rest[c, v, 48:96] = part[1, 128 + 48 * p : 176 + 48 * p]
            rest[c, v, 96:128] = part[2, 256 + 32 * p : 288 + 32 * p]
            rest[c, v, 128:144] = part[3, 384 + 16 * p : 400 + 16 * p]
            rest[c, v, 144:152] = vec_tile

    pl.semaphore_wait(barrier, len(peers))

    first_core = start(first.at[1 - core], first_from.at[0], core_peer)
    rest_core = start(rest.at[1 - core], rest_from.at[0], core_peer)
    first_core.wait()
    first[core] = first[core] + first_from[0]
    first_y = [start(first.at[core, v], first_from.at[1, d], peer(y=v)) for d, v in enumerate(y_at)]
    rest_core.wait()
    rest[core] = rest[core] + rest_from[0]
    rest_y = [start(rest.at[core, v], rest_from.at[1, d], peer(y=v)) for d, v in enumerate(y_at)]
    for copy in first_y:
        copy.wait()
    first_z[0] = (first[core, y] + first_from[1, 0]) + (first_from[1, 1] + first_from[1, 2])
    first_far = start(first_z.at[0], first_z.at[1], z_peer)
    for copy in rest_y:
        copy.wait()
    rest_z[0] = (rest[core, y] + rest_from[1, 0]) + (rest_from[1, 1] + rest_from[1, 2])
    rest_far = start(rest_z.at[0], rest_z.at[1], z_peer)

    first_far.wait()
    first_sum[core, y] = first_z[0] + first_z[1]
    first_y = [start(first_sum.at[core, y], first_sum.at[core, y], peer(y=v)) for v in y_at]
    rest_far.wait()
    rest_sum[core, y] = rest_z[0] + rest_z[1]
    rest_y = [start(rest_sum.at[core, y], rest_sum.at[core, y], peer(y=v)) for v in y_at]
    for copy in first_y:
        copy.wait()
    first_core = start(first_sum.at[core], first_sum.at[core], core_peer)
    for copy in rest_y:
        copy.wait()
    rest_core = start(rest_sum.at[core], rest_sum.at[core], core_peer)
    link[own] = link_ref[...]
    link_far = start(link_ref, link.at[own], z_peer)
    link_near = [start(link_ref, link.at[own], peer(y=v)) for v in y_at]
    first_core.wait()
    a[0, :, :128] = jnp.concatenate([first_sum[p // 4, p % 4] for p in range(8)])
    later = {}

    def between(k):
        if k == 0:
            rest_core.wait()
            spans = ((0, 1, 0, 48), (1, 1, 48, 48), (2, 2, 96, 32), (3, 3, 128, 16))
            for j, i0, low_row, n in spans:
                column = jnp.concatenate([rest_sum[p // 4, p % 4, low_row : low_row + n] for p in range(8)])
                for i in range(i0, 4):
                    block = column[128 * (i - i0) : 128 * (i - i0) + 128]
                    a[i, :, 128 * j : 128 * j + 128] = block
                    if i > j:
                        a[j, :, 128 * i : 128 * i + 128] = block.T
        if k == 1:
            link_far.wait()
            for copy in link_near:
                copy.wait()
            far = pl.ds(pl.multiple_of(32 * ((1 - zh) * 8 + y * 2 + core), 32), 32)
            later["near"] = [start(link.at[far], link.at[far], peer(y=v)) for v in y_at]
        if k == 2:
            for copy in later["near"]:
                copy.wait()
            later["core"] = []
            for n in range(8):
                at = pl.ds(pl.multiple_of(32 * (2 * n + core), 32), 32)
                later["core"].append(start(link.at[at], link.at[at], core_peer))

    inverse_512(a, between)
    for copy in later["core"]:
        copy.wait()
    vec_total = rest_sum[core, y, 144:]

    band = pl.ds(pl.multiple_of(128 * y, 128), 128)
    for n in range(4):
        link_t[:, 128 * n : 128 * n + 128] = link[128 * n : 128 * n + 128, band].T
    z_rows = rows_of(vec_total)
    left[:64] = link_t[pl.ds(pl.multiple_of(64 * core, 64), 64)]
    left[64:] = z_rows

    def by_inverse(v):
        out = dot(v[:, :128], a[0], precision=HIGH)
        for n in range(1, 4):
            out = out + dot(v[:, 128 * n : 128 * n + 128], a[n], precision=HIGH)
        return out

    solved = by_inverse(left[...])
    e_rows = dot(solved, link[...], precision=HIGH)
    w_tile = tile_of(e_rows[64:66])
    for n in range(4):
        e_part[n, :64] = e_rows[:64, 128 * n : 128 * n + 128]
        e_part[n, 64:] = w_tile

    from_x[x] = e_part[x]
    copies = [start(e_part.at[v], from_x.at[x], peer(x=v)) for v in x_at]
    for copy in copies:
        copy.wait()
    from_zl[zl] = (from_x[0] + from_x[1]) + (from_x[2] + from_x[3])
    copies = [start(from_zl.at[zl], from_zl.at[zl], peer(zl=v)) for v in zl_at]
    for n in range(4):
        back[128 * n : 128 * n + 128] = dot(a[n], link[...], precision=HIGH)
    for copy in copies:
        copy.wait()
    summed = from_zl[0]
    for n in range(1, 8):
        summed = summed + from_zl[n]
    s_all[core, y, x] = summed[:64]
    w_sum = rows_of(summed[64:])
    copies = [start(s_all.at[core, y, x], s_all.at[core, y, x], peer(x=v)) for v in x_at]
    for copy in copies:
        copy.wait()
    copies = [start(s_all.at[core, y], s_all.at[core, y], peer(y=v)) for v in y_at]
    for copy in copies:
        copy.wait()
    copy = start(s_all.at[core], s_all.at[core], core_peer)
    loads[6].wait()
    loads[7].wait()
    copy.wait()
    for i in range(4):
        for c in range(2):
            at = slice(64 * c, 64 * c + 64)
            for n in range(4):
                cols = slice(128 * n, 128 * n + 128)
                root[i, at, cols] = s_all[c, i, n] + rdiag[128 * i + 64 * c : 128 * i + 64 * c + 64, cols]
    inverse_512(root)
    q_rows = jnp.concatenate([rrhs_ref[...], jnp.zeros((6, 512), F32)])
    v = w_sum - q_rows
    root_sol = dot(v[:, :128], root[0], precision=HIGH)
    for n in range(1, 4):
        root_sol = root_sol + dot(v[:, 128 * n : 128 * n + 128], root[n], precision=HIGH)
    node_sol = solved[64:] - dot(root_sol, back[...], ((1,), (1,)), precision=HIGH)
    for n in range(16):
        x_rows[n] = node_sol[:2, 32 * n : 32 * n + 32]
    update = dot(node_sol.astype(BF16), reduced[...])
    difference = (update - projected[...]).astype(BF16)
    out_ref[0:2] = dot(difference, factor[...], ((1,), (1,)))[:2]
    out_ref[2:4, :512] = root_sol[:2]
    out_ref[4:6, :32] = x_rows[scen]


def parted(all_ref, leaf_ref, node_ref, root_ref):
    leaf_ref[...] = all_ref[0:2]
    root_ref[...] = all_ref[2:4, :512]
    node_ref[...] = all_ref[4:6, :32]


def local(factors, couple, leaf_rhs, node_diag, node_rhs, link_root, root_diag, root_rhs):
    vmem, hbm = pl.BlockSpec(memory_space=pltpu.VMEM), pl.BlockSpec(memory_space=pl.ANY)
    copies = 64
    everything = pl.pallas_call(
        body,
        out_shape=jax.ShapeDtypeStruct((8, 1024), F32),
        in_specs=[hbm] * 8,
        out_specs=vmem,
        scratch_shapes=[
            pltpu.VMEM((1024, 1024), BF16),
            pltpu.VMEM((1024, 512), BF16),
            pltpu.VMEM((2, 1024), BF16),
            pltpu.VMEM((32, 512), F32),
            pltpu.VMEM((2, 32), F32),
            pltpu.VMEM((32, 512), F32),
            pltpu.VMEM((512, 512), F32),
            pltpu.VMEM((2, 512), F32),
            pltpu.VMEM((512, 1024), BF16),
            pltpu.VMEM((8, 1024), F32),
            pltpu.VMEM((4, 512, 128), F32),
            pltpu.VMEM((2, 4, 16, 128), F32),
            pltpu.VMEM((2, 4, 16, 128), F32),
            pltpu.VMEM((2, 16, 128), F32),
            pltpu.VMEM((2, 4, 16, 128), F32),
            pltpu.VMEM((2, 4, 152, 128), F32),
            pltpu.VMEM((2, 4, 152, 128), F32),
            pltpu.VMEM((2, 152, 128), F32),
            pltpu.VMEM((2, 4, 152, 128), F32),
            pltpu.VMEM((512, 512), F32),
            pltpu.VMEM((128, 512), F32),
            pltpu.VMEM((4, 128, 512), F32),
            pltpu.VMEM((72, 512), F32),
            pltpu.VMEM((4, 72, 128), F32),
            pltpu.VMEM((4, 72, 128), F32),
            pltpu.VMEM((8, 72, 128), F32),
            pltpu.VMEM((512, 512), F32),
            pltpu.VMEM((2, 4, 4, 64, 128), F32),
            pltpu.VMEM((4, 128, 512), F32),
            pltpu.VMEM((16, 2, 32), F32),
            pltpu.SemaphoreType.DMA((copies,)),
            pltpu.SemaphoreType.DMA((copies,)),
            pltpu.SemaphoreType.DMA((8,)),
        ],
        compiler_params=pltpu.CompilerParams(
            collective_id=0, has_side_effects=True, vmem_limit_bytes=60 * 1024 * 1024
        ),
        name="newton",
    )(factors[0, 0], couple[0, 0], leaf_rhs[0, 0], node_diag[0], node_rhs[0], link_root[0], root_diag, root_rhs)
    leaf, node, root = pl.pallas_call(
        parted,
        out_shape=(
            jax.ShapeDtypeStruct((2, 1024), F32),
            jax.ShapeDtypeStruct((2, 32), F32),
            jax.ShapeDtypeStruct((2, 512), F32),
        ),
        in_specs=[vmem],
        out_specs=(vmem, vmem, vmem),
        name="parted",
    )(everything)
    return (leaf[None, None], node[None], root)


def solution(mesh):
    torus = Mesh(mesh.devices.reshape(2, 4, 2, 4, 8), AXES)
    scen, node = ("zh", "y", "core"), ("x", "zl")
    placed = (
        P(node, scen, None, None),
        P(node, scen, None, None),
        P(node, scen, None, None),
        P(node, scen, None),
        P(node, None, scen),
        P(node, scen, None),
        P(),
        P(),
    )
    return jax.shard_map(
        local,
        mesh=torus,
        in_specs=placed,
        out_specs=(P(node, scen, None, None), P(node, None, scen), P()),
        check_vma=False,
    )
```

```python
import jax
import jax.numpy as jnp
from jax import lax
from jax.experimental import pallas as pl
from jax.experimental.pallas import tpu as pltpu
from jax.sharding import Mesh
from jax.sharding import PartitionSpec as P

AXES = ("zh", "y", "core", "x", "zl")
MESH = pl.DeviceIdType.MESH
HIGH = lax.Precision.HIGHEST
F32 = jnp.float32
BF16 = jnp.bfloat16


def dot(a, b, dims=((1,), (0,)), precision=None):
    return lax.dot_general(a, b, (dims, ((), ())), precision=precision, preferred_element_type=F32)


def thirds(v):
    high = v.astype(BF16).astype(F32)
    mid = (v - high).astype(BF16).astype(F32)
    return high, mid, v - high - mid


def inverse_128(a, work=()):
    rows = lax.broadcasted_iota(jnp.int32, (8, 128), 0)
    lanes = lax.broadcasted_iota(jnp.int32, (8, 128), 1)
    wide_lanes = lax.broadcasted_iota(jnp.int32, (128, 128), 1)
    work = list(work)
    following = a[:8]
    for s in range(16):
        at = 8 * s
        panel = following
        ah, am, al = thirds(jnp.where(lanes < at, -panel, panel))
        cols = jnp.stack([jnp.broadcast_to(panel[:, at + j : at + j + 1], (8, 128)) for j in range(8)])
        here = (lanes >= at) & (lanes < at + 8)
        panel = jnp.where(here, jnp.where(lanes - at == rows, 1.0, 0.0), panel)
        for j in range(8):
            mine = rows == j
            col = cols[0]
            inv = pl.reciprocal(jnp.broadcast_to(col[j : j + 1], (8, 128)), approx=True)
            f = jnp.where(mine, -inv, col * inv)
            if j < 7:
                rest = cols[1:]
                pivot = jnp.broadcast_to(rest[:, j : j + 1], rest.shape)
                cols = jnp.where(mine[None], 0.0, rest) - f[None] * pivot
            panel = jnp.where(mine, 0.0, panel) - f * jnp.broadcast_to(panel[j : j + 1], (8, 128))
        if s < 15:
            old = a[at + 8 : at + 16]
            following = jnp.where(here, 0.0, old)
            for j in range(8):
                following = following - jnp.broadcast_to(old[:, at + j : at + j + 1], (8, 128)) * jnp.broadcast_to(
                    panel[j : j + 1], (8, 128)
                )
        bh, bm, bl = thirds(panel)
        left = jnp.concatenate([ah, ah, ah, am, am, al]).astype(BF16)
        right = jnp.concatenate([bh, bm, bl, bh, bm, bh]).astype(BF16)
        new = jnp.where((wide_lanes >= at) & (wide_lanes < at + 8), 0.0, a) - dot(left, right, ((0,), (0,)))
        a = jnp.concatenate([part for part in (new[:at], panel, new[at + 8 :]) if part.shape[0]])
        for _ in range(-(-len(work) // (16 - s))):
            work.pop(0)()
    return a


def inverse_512(a, between=None):
    work = []
    cols = [slice(128 * n, 128 * n + 128) for n in range(4)]
    for k in range(4):
        inv = inverse_128(a[k, :, cols[k]], work)
        if between is not None:
            between(k)
        work = []
        nxt = k + 1
        def row(j, k=k, inv=inv):
            a[k, :, cols[j]] = dot(inv, a[k, :, cols[j]], precision=HIGH)
        def update(i, j, k=k):
            a[i, :, cols[j]] = a[i, :, cols[j]] - dot(a[i, :, cols[k]], a[k, :, cols[j]], precision=HIGH)
        def column(i, k=k, inv=inv):
            a[i, :, cols[k]] = -dot(a[i, :, cols[k]], inv, precision=HIGH)
        others = [n for n in range(4) if n != k]
        if nxt < 4:
            row(nxt); update(nxt, nxt)
        for j in others:
            if j != nxt: work.append(lambda j=j, f=row: f(j))
        for j in others:
            for i in others:
                if not (i == j == nxt): work.append(lambda i=i, j=j, f=update: f(i, j))
        for i in others: work.append(lambda i=i, f=column: f(i))
        def keep(k=k, inv=inv):
            a[k, :, cols[k]] = inv

        work.append(keep)
    for w in work:
        w()


def tile_of(vec):
    return jnp.concatenate([vec[:, 128 * j : 128 * j + 128] for j in range(4)])


def rows_of(tile):
    vec = jnp.concatenate([tile[2 * j : 2 * j + 2] for j in range(4)], axis=1)
    return jnp.concatenate([vec, jnp.zeros((6, 512), F32)])


def body(
    factor_hbm, couple_hbm, rights_hbm, diag_hbm, nrhs_hbm, link_hbm, rdiag_hbm, rrhs_hbm,
    out_ref,
    factor, coupling, rights_ref, diag_ref, nrhs_ref, link_ref, rdiag, rrhs_ref, reduced, projected, part, first, first_from, first_z, first_sum,
    rest, rest_from, rest_z, rest_sum, link, link_t, a, left, e_blocks, e_part, from_x, from_zl, back, s_all, root, v_blocks, x_blocks, x_rows,
    send, recv, load,
):
    zh, y, core, x, zl = (lax.axis_index(n) for n in AXES)
    scen = zh * 8 + y * 2 + core

    def peer(**at):
        here = dict(zh=zh, y=y, core=core, x=x, zl=zl)
        here.update(at)
        return tuple(here[n] for n in AXES)

    z_peer, core_peer = peer(zh=1 - zh), peer(core=1 - core)
    y_at = [lax.rem(y + d, 4) for d in range(1, 4)]
    x_at = [lax.rem(x + d, 4) for d in range(1, 4)]
    zl_at = [lax.rem(zl + d, 8) for d in range(1, 8)]
    peers = [z_peer, core_peer] + [peer(y=v) for v in y_at] + [peer(x=v) for v in x_at] + [peer(zl=v) for v in zl_at]
    barrier = pltpu.get_barrier_semaphore()
    for device in peers:
        pl.semaphore_signal(barrier, 1, device_id=device, device_id_type=MESH)

    loads = [
        pltpu.make_async_copy(src, dst, load.at[n])
        for n, (src, dst) in enumerate(
            (
                (couple_hbm, coupling),
                (factor_hbm, factor),
                (rights_hbm, rights_ref),
                (diag_hbm, diag_ref),
                (nrhs_hbm, nrhs_ref),
                (link_hbm, link_ref),
                (rdiag_hbm, rdiag),
                (rrhs_hbm, rrhs_ref),
            )
        )
    ]
    for copy in loads:
        copy.start()

    used = [0]

    def start(src, dst, device):
        n = used[0]
        used[0] += 1
        copy = pltpu.make_async_remote_copy(
            src_ref=src, dst_ref=dst, send_sem=send.at[n], recv_sem=recv.at[n], device_id=device, device_id_type=MESH
        )
        copy.start()
        return copy

    for n in range(6):
        loads[n].wait()
    rights = jnp.concatenate([rights_ref[...].astype(F32), jnp.zeros((6, 1024), F32)]).astype(BF16)
    reduced[...] = dot(coupling[...], factor[...], ((0,), (0,))).astype(BF16)
    projected[...] = dot(rights, factor[...])
    for j in range(4):
        part[j, 128 * j :] = dot(reduced[128 * j :], reduced[128 * j : 128 * j + 128], ((1,), (1,)))
    low = projected[...].astype(BF16)
    vec = dot(low, reduced[...], ((1,), (1,)))
    own = pl.ds(pl.multiple_of(32 * scen, 32), 32)
    for j in range(4):
        part[j, own] = part[j, own] + diag_ref[:, 128 * j : 128 * j + 128]
    rows = lax.broadcasted_iota(jnp.int32, (8, 128), 0)
    lanes = lax.broadcasted_iota(jnp.int32, (8, 128), 1)
    strip = jnp.concatenate([nrhs_ref[...]] * 4, axis=1)
    strip = jnp.concatenate([strip] * 4)
    mine = (rows // 2 == scen // 4) & (lanes // 32 == lax.rem(scen, 4))
    vec_tile = tile_of(vec[:2]) + jnp.where(mine, strip, 0.0)
    for c in range(2):
        for v in range(4):
            p = 4 * c + v
            first[c, v] = part[0, 16 * p : 16 * p + 16]
            rest[c, v, 0:48] = part[0, 128 + 48 * p : 176 + 48 * p]
            rest[c, v, 48:96] = part[1, 128 + 48 * p : 176 + 48 * p]
            rest[c, v, 96:128] = part[2, 256 + 32 * p : 288 + 32 * p]
            rest[c, v, 128:144] = part[3, 384 + 16 * p : 400 + 16 * p]
            rest[c, v, 144:152] = vec_tile

    pl.semaphore_wait(barrier, len(peers))

    first_core = start(first.at[1 - core], first_from.at[0], core_peer)
    rest_core = start(rest.at[1 - core], rest_from.at[0], core_peer)
    first_core.wait()
    first[core] = first[core] + first_from[0]
    first_y = [start(first.at[core, v], first_from.at[1, d], peer(y=v)) for d, v in enumerate(y_at)]
    rest_core.wait()
    rest[core] = rest[core] + rest_from[0]
    rest_y = [start(rest.at[core, v], rest_from.at[1, d], peer(y=v)) for d, v in enumerate(y_at)]
    for copy in first_y:
        copy.wait()
    first_z[0] = (first[core, y] + first_from[1, 0]) + (first_from[1, 1] + first_from[1, 2])
    first_far = start(first_z.at[0], first_z.at[1], z_peer)
    for copy in rest_y:
        copy.wait()
    rest_z[0] = (rest[core, y] + rest_from[1, 0]) + (rest_from[1, 1] + rest_from[1, 2])
    rest_far = start(rest_z.at[0], rest_z.at[1], z_peer)

    first_far.wait()
    first_sum[core, y] = first_z[0] + first_z[1]
    first_y = [start(first_sum.at[core, y], first_sum.at[core, y], peer(y=v)) for v in y_at]
    rest_far.wait()
    rest_sum[core, y] = rest_z[0] + rest_z[1]
    rest_y = [start(rest_sum.at[core, y], rest_sum.at[core, y], peer(y=v)) for v in y_at]
    for copy in first_y:
        copy.wait()
    first_core = start(first_sum.at[core], first_sum.at[core], core_peer)
    for copy in rest_y:
        copy.wait()
    rest_core = start(rest_sum.at[core], rest_sum.at[core], core_peer)
    link[own] = link_ref[...]
    link_far = start(link_ref, link.at[own], z_peer)
    link_near = [start(link_ref, link.at[own], peer(y=v)) for v in y_at]
    first_core.wait()
    a[0, :, :128] = jnp.concatenate([first_sum[p // 4, p % 4] for p in range(8)])
    later = {}

    def between(k):
        if k == 0:
            rest_core.wait()
            spans = ((0, 1, 0, 48), (1, 1, 48, 48), (2, 2, 96, 32), (3, 3, 128, 16))
            for j, i0, low_row, n in spans:
                column = jnp.concatenate([rest_sum[p // 4, p % 4, low_row : low_row + n] for p in range(8)])
                for i in range(i0, 4):
                    block = column[128 * (i - i0) : 128 * (i - i0) + 128]
                    a[i, :, 128 * j : 128 * j + 128] = block
                    if i > j:
                        a[j, :, 128 * i : 128 * i + 128] = block.T
        if k == 1:
            link_far.wait()
            for copy in link_near:
                copy.wait()
            far = pl.ds(pl.multiple_of(32 * ((1 - zh) * 8 + y * 2 + core), 32), 32)
            later["near"] = [start(link.at[far], link.at[far], peer(y=v)) for v in y_at]
        if k == 2:
            for copy in later["near"]:
                copy.wait()
            later["core"] = []
            for n in range(8):
                at = pl.ds(pl.multiple_of(32 * (2 * n + core), 32), 32)
                later["core"].append(start(link.at[at], link.at[at], core_peer))

    inverse_512(a, between)
    for copy in later["core"]:
        copy.wait()
    vec_total = rest_sum[core, y, 144:]

    band = pl.ds(pl.multiple_of(128 * y, 128), 128)
    for n in range(4):
        link_t[:, 128 * n : 128 * n + 128] = link[128 * n : 128 * n + 128, band].T
    z_rows = rows_of(vec_total)
    left[:64] = link_t[pl.ds(pl.multiple_of(64 * core, 64), 64)]
    left[64:] = z_rows

    def by_inverse(v):
        out = dot(v[:, :128], a[0], precision=HIGH)
        for n in range(1, 4):
            out = out + dot(v[:, 128 * n : 128 * n + 128], a[n], precision=HIGH)
        return out

    solved = by_inverse(left[...])
    e_rows = dot(solved, link[...], precision=HIGH)
    w_tile = tile_of(e_rows[64:66])
    for n in range(4):
        e_blocks[n] = e_rows[:64, 128 * n : 128 * n + 128]
    for q in range(3):
        block = e_blocks[lax.rem(y + q, 4)]
        for n in range(4):
            e_part[n, 16 * q : 16 * q + 16] = block[16 * n : 16 * n + 16]
    for n in range(4):
        e_part[n, 48:] = w_tile

    from_x[x] = e_part[x]
    copies = [start(e_part.at[v], from_x.at[x], peer(x=v)) for v in x_at]
    for copy in copies:
        copy.wait()
    from_zl[zl] = (from_x[0] + from_x[1]) + (from_x[2] + from_x[3])
    copies = [start(from_zl.at[zl], from_zl.at[zl], peer(zl=v)) for v in zl_at]
    for n in range(4):
        back[128 * n : 128 * n + 128] = dot(a[n], link[...], precision=HIGH)
    for copy in copies:
        copy.wait()
    summed = from_zl[0]
    for n in range(1, 8):
        summed = summed + from_zl[n]
    s_all[core, y, x] = summed[:48]
    w_sum = rows_of(summed[48:])
    copies = [start(s_all.at[core, y, x], s_all.at[core, y, x], peer(x=v)) for v in x_at]
    for n in (6, 7):
        loads[n].wait()
    v = w_sum - jnp.concatenate([rrhs_ref[...], jnp.zeros((6, 512), F32)])
    for n in range(4):
        v_blocks[n] = v[:, 128 * n : 128 * n + 128]
    for copy in copies:
        copy.wait()
    own_block = start(s_all.at[core, y], s_all.at[core, y], core_peer)
    other_blocks = [start(s_all.at[core, y], s_all.at[core, y], peer(y=v)) for v in y_at]

    turn = [y] + y_at

    def spot(t):
        return pl.ds(pl.multiple_of(128 * turn[t % 4], 128), 128)

    def place(t, q):
        block = jnp.concatenate([s_all[n // 4, turn[t], n % 4, 16 * q : 16 * q + 16] for n in range(8)])
        u = (t + q) % 4
        root[t, :, 128 * u : 128 * u + 128] = block + rdiag[spot(t), spot(u)]
        if q == 1:
            root[u, :, 128 * t : 128 * t + 128] = block.T + rdiag[spot(u), spot(t)]

    def between_root(k):
        if k == 0:
            forward = []
            for copy, v in zip(other_blocks, reversed(y_at)):
                copy.wait()
                forward.append(start(s_all.at[core, v], s_all.at[core, v], core_peer))
            place(0, 1)
            place(0, 2)
            for copy in forward:
                copy.wait()
            for t in range(1, 4):
                for q in range(3):
                    place(t, q)

    own_block.wait()
    place(0, 0)
    inverse_512(root, between_root)
    turned = dot(v_blocks[turn[0]], root[0], precision=HIGH)
    for t in range(1, 4):
        turned = turned + dot(v_blocks[turn[t]], root[t], precision=HIGH)
    for t in range(4):
        x_blocks[turn[t]] = turned[:, 128 * t : 128 * t + 128]
    root_sol = jnp.concatenate([x_blocks[n] for n in range(4)], axis=1)
    node_sol = solved[64:] - dot(root_sol, back[...], ((1,), (1,)), precision=HIGH)
    for n in range(16):
        x_rows[n] = node_sol[:2, 32 * n : 32 * n + 32]
    update = dot(node_sol.astype(BF16), reduced[...])
    difference = (update - projected[...]).astype(BF16)
    out_ref[0:2] = dot(difference, factor[...], ((1,), (1,)))[:2]
    out_ref[2:4, :512] = root_sol[:2]
    out_ref[4:6, :32] = x_rows[scen]


def parted(all_ref, leaf_ref, node_ref, root_ref):
    leaf_ref[...] = all_ref[0:2]
    root_ref[...] = all_ref[2:4, :512]
    node_ref[...] = all_ref[4:6, :32]


def local(factors, couple, leaf_rhs, node_diag, node_rhs, link_root, root_diag, root_rhs):
    vmem, hbm = pl.BlockSpec(memory_space=pltpu.VMEM), pl.BlockSpec(memory_space=pl.ANY)
    copies = 64
    everything = pl.pallas_call(
        body,
        out_shape=jax.ShapeDtypeStruct((8, 1024), F32),
        in_specs=[hbm] * 8,
        out_specs=vmem,
        scratch_shapes=[
            pltpu.VMEM((1024, 1024), BF16),
            pltpu.VMEM((1024, 512), BF16),
            pltpu.VMEM((2, 1024), BF16),
            pltpu.VMEM((32, 512), F32),
            pltpu.VMEM((2, 32), F32),
            pltpu.VMEM((32, 512), F32),
            pltpu.VMEM((512, 512), F32),
            pltpu.VMEM((2, 512), F32),
            pltpu.VMEM((512, 1024), BF16),
            pltpu.VMEM((8, 1024), F32),
            pltpu.VMEM((4, 512, 128), F32),
            pltpu.VMEM((2, 4, 16, 128), F32),
            pltpu.VMEM((2, 4, 16, 128), F32),
            pltpu.VMEM((2, 16, 128), F32),
            pltpu.VMEM((2, 4, 16, 128), F32),
            pltpu.VMEM((2, 4, 152, 128), F32),
            pltpu.VMEM((2, 4, 152, 128), F32),
            pltpu.VMEM((2, 152, 128), F32),
            pltpu.VMEM((2, 4, 152, 128), F32),
            pltpu.VMEM((512, 512), F32),
            pltpu.VMEM((128, 512), F32),
            pltpu.VMEM((4, 128, 512), F32),
            pltpu.VMEM((72, 512), F32),
            pltpu.VMEM((4, 64, 128), F32),
            pltpu.VMEM((4, 56, 128), F32),
            pltpu.VMEM((4, 56, 128), F32),
            pltpu.VMEM((8, 56, 128), F32),
            pltpu.VMEM((512, 512), F32),
            pltpu.VMEM((2, 4, 4, 48, 128), F32),
            pltpu.VMEM((4, 128, 512), F32),
            pltpu.VMEM((4, 8, 128), F32),
            pltpu.VMEM((4, 8, 128), F32),
            pltpu.VMEM((16, 2, 32), F32),
            pltpu.SemaphoreType.DMA((copies,)),
            pltpu.SemaphoreType.DMA((copies,)),
            pltpu.SemaphoreType.DMA((8,)),
        ],
        compiler_params=pltpu.CompilerParams(
            collective_id=0, has_side_effects=True, vmem_limit_bytes=60 * 1024 * 1024
        ),
        name="newton",
    )(factors[0, 0], couple[0, 0], leaf_rhs[0, 0], node_diag[0], node_rhs[0], link_root[0], root_diag, root_rhs)
    leaf, node, root = pl.pallas_call(
        parted,
        out_shape=(
            jax.ShapeDtypeStruct((2, 1024), F32),
            jax.ShapeDtypeStruct((2, 32), F32),
            jax.ShapeDtypeStruct((2, 512), F32),
        ),
        in_specs=[vmem],
        out_specs=(vmem, vmem, vmem),
        name="parted",
    )(everything)
    return (leaf[None, None], node[None], root)


def solution(mesh):
    torus = Mesh(mesh.devices.reshape(2, 4, 2, 4, 8), AXES)
    scen, node = ("zh", "y", "core"), ("x", "zl")
    placed = (
        P(node, scen, None, None),
        P(node, scen, None, None),
        P(node, scen, None, None),
        P(node, scen, None),
        P(node, None, scen),
        P(node, scen, None),
        P(),
        P(),
    )
    return jax.shard_map(
        local,
        mesh=torus,
        in_specs=placed,
        out_specs=(P(node, scen, None, None), P(node, None, scen), P()),
        check_vma=False,
    )
```

```python
import jax
import jax.numpy as jnp
from jax import lax
from jax.experimental import pallas as pl
from jax.experimental.pallas import tpu as pltpu
from jax.sharding import Mesh
from jax.sharding import PartitionSpec as P

AXES = ("zh", "y", "core", "x", "zl")
MESH = pl.DeviceIdType.MESH
HIGH = lax.Precision.HIGHEST
F32 = jnp.float32
BF16 = jnp.bfloat16


def dot(a, b, dims=((1,), (0,)), precision=None):
    return lax.dot_general(a, b, (dims, ((), ())), precision=precision, preferred_element_type=F32)


def thirds(v):
    high = v.astype(BF16).astype(F32)
    mid = (v - high).astype(BF16).astype(F32)
    return high, mid, v - high - mid


def inverse_128(a, work=()):
    rows = lax.broadcasted_iota(jnp.int32, (8, 128), 0)
    lanes = lax.broadcasted_iota(jnp.int32, (8, 128), 1)
    wide_lanes = lax.broadcasted_iota(jnp.int32, (128, 128), 1)
    work = list(work)
    following = a[:8]
    for s in range(16):
        at = 8 * s
        panel = following
        ah, am, al = thirds(jnp.where(lanes < at, -panel, panel))
        cols = jnp.stack([jnp.broadcast_to(panel[:, at + j : at + j + 1], (8, 128)) for j in range(8)])
        here = (lanes >= at) & (lanes < at + 8)
        panel = jnp.where(here, jnp.where(lanes - at == rows, 1.0, 0.0), panel)
        for j in range(8):
            mine = rows == j
            col = cols[0]
            inv = pl.reciprocal(jnp.broadcast_to(col[j : j + 1], (8, 128)), approx=True)
            f = jnp.where(mine, -inv, col * inv)
            if j < 7:
                rest = cols[1:]
                pivot = jnp.broadcast_to(rest[:, j : j + 1], rest.shape)
                cols = jnp.where(mine[None], 0.0, rest) - f[None] * pivot
            panel = jnp.where(mine, 0.0, panel) - f * jnp.broadcast_to(panel[j : j + 1], (8, 128))
        if s < 15:
            old = a[at + 8 : at + 16]
            following = jnp.where(here, 0.0, old)
            for j in range(8):
                following = following - jnp.broadcast_to(old[:, at + j : at + j + 1], (8, 128)) * jnp.broadcast_to(
                    panel[j : j + 1], (8, 128)
                )
        bh, bm, bl = thirds(panel)
        left = jnp.concatenate([ah, ah, ah, am, am, al]).astype(BF16)
        right = jnp.concatenate([bh, bm, bl, bh, bm, bh]).astype(BF16)
        new = jnp.where((wide_lanes >= at) & (wide_lanes < at + 8), 0.0, a) - dot(left, right, ((0,), (0,)))
        a = jnp.concatenate([part for part in (new[:at], panel, new[at + 8 :]) if part.shape[0]])
        for _ in range(-(-len(work) // (16 - s))):
            work.pop(0)()
    return a


def inverse_512(a, between=None):
    work = []
    cols = [slice(128 * n, 128 * n + 128) for n in range(4)]
    for k in range(4):
        inv = inverse_128(a[k, :, cols[k]], work)
        if between is not None:
            between(k)
        work = []
        nxt = k + 1
        def row(j, k=k, inv=inv):
            a[k, :, cols[j]] = dot(inv, a[k, :, cols[j]], precision=HIGH)
        def update(i, j, k=k):
            a[i, :, cols[j]] = a[i, :, cols[j]] - dot(a[i, :, cols[k]], a[k, :, cols[j]], precision=HIGH)
        def column(i, k=k, inv=inv):
            a[i, :, cols[k]] = -dot(a[i, :, cols[k]], inv, precision=HIGH)
        others = [n for n in range(4) if n != k]
        if nxt < 4:
            row(nxt); update(nxt, nxt)
        for j in others:
            if j != nxt: work.append(lambda j=j, f=row: f(j))
        for j in others:
            for i in others:
                if not (i == j == nxt): work.append(lambda i=i, j=j, f=update: f(i, j))
        for i in others: work.append(lambda i=i, f=column: f(i))
        def keep(k=k, inv=inv):
            a[k, :, cols[k]] = inv

        work.append(keep)
    for w in work:
        w()


def tile_of(vec):
    return jnp.concatenate([vec[:, 128 * j : 128 * j + 128] for j in range(4)])


def rows_of(tile):
    vec = jnp.concatenate([tile[2 * j : 2 * j + 2] for j in range(4)], axis=1)
    return jnp.concatenate([vec, jnp.zeros((6, 512), F32)])


def body(
    factor_hbm, couple_hbm, rights_hbm, diag_hbm, nrhs_hbm, link_hbm, rdiag_hbm, rrhs_hbm,
    out_ref,
    factor, coupling, rights_ref, diag_ref, nrhs_ref, link_ref, rdiag, rrhs_ref, reduced, projected, part, first, first_from, first_z, first_sum,
    rest, rest_from, rest_z, rest_sum, link, link_t, a, left, e_blocks, e_part, from_x, from_zl, back, s_all, root, v_blocks, x_blocks, x_rows,
    send, recv, load,
):
    zh, y, core, x, zl = (lax.axis_index(n) for n in AXES)
    scen = zh * 8 + y * 2 + core

    def peer(**at):
        here = dict(zh=zh, y=y, core=core, x=x, zl=zl)
        here.update(at)
        return tuple(here[n] for n in AXES)

    z_peer, core_peer = peer(zh=1 - zh), peer(core=1 - core)
    y_at = [lax.rem(y + d, 4) for d in range(1, 4)]
    x_at = [lax.rem(x + d, 4) for d in range(1, 4)]
    zl_at = [lax.rem(zl + d, 8) for d in range(1, 8)]
    peers = [z_peer, core_peer] + [peer(y=v) for v in y_at] + [peer(x=v) for v in x_at] + [peer(zl=v) for v in zl_at]
    barrier = pltpu.get_barrier_semaphore()
    for device in peers:
        pl.semaphore_signal(barrier, 1, device_id=device, device_id_type=MESH)

    loads = [
        pltpu.make_async_copy(src, dst, load.at[n])
        for n, (src, dst) in enumerate(
            (
                (couple_hbm, coupling),
                (factor_hbm, factor),
                (rights_hbm, rights_ref),
                (diag_hbm, diag_ref),
                (nrhs_hbm, nrhs_ref),
                (link_hbm, link_ref),
                (rdiag_hbm, rdiag),
                (rrhs_hbm, rrhs_ref),
            )
        )
    ]
    for copy in loads:
        copy.start()

    used = [0]

    def start(src, dst, device):
        n = used[0]
        used[0] += 1
        copy = pltpu.make_async_remote_copy(
            src_ref=src, dst_ref=dst, send_sem=send.at[n], recv_sem=recv.at[n], device_id=device, device_id_type=MESH
        )
        copy.start()
        return copy

    for n in range(6):
        loads[n].wait()
    rights = jnp.concatenate([rights_ref[...].astype(F32), jnp.zeros((6, 1024), F32)]).astype(BF16)
    reduced[...] = dot(coupling[...], factor[...], ((0,), (0,))).astype(BF16)
    projected[...] = dot(rights, factor[...])
    for j in range(4):
        part[j, 128 * j :] = dot(reduced[128 * j :], reduced[128 * j : 128 * j + 128], ((1,), (1,)))
    low = projected[...].astype(BF16)
    vec = dot(low, reduced[...], ((1,), (1,)))
    own = pl.ds(pl.multiple_of(32 * scen, 32), 32)
    for j in range(4):
        part[j, own] = part[j, own] + diag_ref[:, 128 * j : 128 * j + 128]
    rows = lax.broadcasted_iota(jnp.int32, (8, 128), 0)
    lanes = lax.broadcasted_iota(jnp.int32, (8, 128), 1)
    strip = jnp.concatenate([nrhs_ref[...]] * 4, axis=1)
    strip = jnp.concatenate([strip] * 4)
    mine = (rows // 2 == scen // 4) & (lanes // 32 == lax.rem(scen, 4))
    vec_tile = tile_of(vec[:2]) + jnp.where(mine, strip, 0.0)
    for c in range(2):
        for v in range(4):
            p = 4 * c + v
            first[c, v] = part[0, 16 * p : 16 * p + 16]
            rest[c, v, 0:48] = part[0, 128 + 48 * p : 176 + 48 * p]
            rest[c, v, 48:96] = part[1, 128 + 48 * p : 176 + 48 * p]
            rest[c, v, 96:128] = part[2, 256 + 32 * p : 288 + 32 * p]
            rest[c, v, 128:144] = part[3, 384 + 16 * p : 400 + 16 * p]
            rest[c, v, 144:152] = vec_tile

    pl.semaphore_wait(barrier, len(peers))

    first_core = start(first.at[1 - core], first_from.at[0], core_peer)
    rest_core = start(rest.at[1 - core], rest_from.at[0], core_peer)
    first_core.wait()
    first[core] = first[core] + first_from[0]
    first_y = [start(first.at[core, v], first_from.at[1, d], peer(y=v)) for d, v in enumerate(y_at)]
    rest_core.wait()
    rest[core] = rest[core] + rest_from[0]
    rest_y = [start(rest.at[core, v], rest_from.at[1, d], peer(y=v)) for d, v in enumerate(y_at)]
    for copy in first_y:
        copy.wait()
    first_z[0] = (first[core, y] + first_from[1, 0]) + (first_from[1, 1] + first_from[1, 2])
    first_far = start(first_z.at[0], first_z.at[1], z_peer)
    for copy in rest_y:
        copy.wait()
    rest_z[0] = (rest[core, y] + rest_from[1, 0]) + (rest_from[1, 1] + rest_from[1, 2])
    rest_far = start(rest_z.at[0], rest_z.at[1], z_peer)

    first_far.wait()
    first_sum[core, y] = first_z[0] + first_z[1]
    first_y = [start(first_sum.at[core, y], first_sum.at[core, y], peer(y=v)) for v in y_at]
    for copy in first_y:
        copy.wait()
    first_core = start(first_sum.at[core], first_sum.at[core], core_peer)
    rest_far.wait()
    rest_sum[core, y] = rest_z[0] + rest_z[1]
    rest_y = [start(rest_sum.at[core, y], rest_sum.at[core, y], peer(y=v)) for v in y_at]
    rest_core = [start(rest_sum.at[core, y], rest_sum.at[core, y], core_peer)]
    link[own] = link_ref[...]
    link_far = start(link_ref, link.at[own], z_peer)
    first_core.wait()
    a[0, :, :128] = jnp.concatenate([first_sum[p // 4, p % 4] for p in range(8)])
    later = {}

    def between(k):
        if k == 0:
            for copy, v in zip(rest_y, reversed(y_at)):
                copy.wait()
                rest_core.append(start(rest_sum.at[core, v], rest_sum.at[core, v], core_peer))
            later["own"] = [start(link_ref, link.at[own], peer(y=v)) for v in y_at]
            for copy in rest_core:
                copy.wait()
            spans = ((0, 1, 0, 48), (1, 1, 48, 48), (2, 2, 96, 32), (3, 3, 128, 16))
            for j, i0, low_row, n in spans:
                column = jnp.concatenate([rest_sum[p // 4, p % 4, low_row : low_row + n] for p in range(8)])
                for i in range(i0, 4):
                    block = column[128 * (i - i0) : 128 * (i - i0) + 128]
                    a[i, :, 128 * j : 128 * j + 128] = block
                    if i > j:
                        a[j, :, 128 * i : 128 * i + 128] = block.T
        if k == 1:
            link_far.wait()
            for copy in later["own"]:
                copy.wait()
            far = pl.ds(pl.multiple_of(32 * ((1 - zh) * 8 + y * 2 + core), 32), 32)
            later["near"] = [start(link.at[far], link.at[far], peer(y=v)) for v in y_at]
        if k == 2:
            for copy in later["near"]:
                copy.wait()
            later["core"] = []
            for n in range(8):
                at = pl.ds(pl.multiple_of(32 * (2 * n + core), 32), 32)
                later["core"].append(start(link.at[at], link.at[at], core_peer))

    inverse_512(a, between)
    for copy in later["core"]:
        copy.wait()
    vec_total = rest_sum[core, y, 144:]

    band = pl.ds(pl.multiple_of(128 * y, 128), 128)
    for n in range(4):
        link_t[:, 128 * n : 128 * n + 128] = link[128 * n : 128 * n + 128, band].T
    z_rows = rows_of(vec_total)
    left[:64] = link_t[pl.ds(pl.multiple_of(64 * core, 64), 64)]
    left[64:] = z_rows

    def by_inverse(v):
        out = dot(v[:, :128], a[0], precision=HIGH)
        for n in range(1, 4):
            out = out + dot(v[:, 128 * n : 128 * n + 128], a[n], precision=HIGH)
        return out

    solved = by_inverse(left[...])
    e_rows = dot(solved, link[...], precision=HIGH)
    w_tile = tile_of(e_rows[64:66])
    for n in range(4):
        e_blocks[n] = e_rows[:64, 128 * n : 128 * n + 128]
    for q in range(3):
        block = e_blocks[lax.rem(y + q, 4)]
        for n in range(4):
            e_part[n, 16 * q : 16 * q + 16] = block[16 * n : 16 * n + 16]
    for n in range(4):
        e_part[n, 48:] = w_tile

    from_x[x] = e_part[x]
    copies = [start(e_part.at[v], from_x.at[x], peer(x=v)) for v in x_at]
    for copy in copies:
        copy.wait()
    from_zl[zl] = (from_x[0] + from_x[1]) + (from_x[2] + from_x[3])
    copies = [start(from_zl.at[zl], from_zl.at[zl], peer(zl=v)) for v in zl_at]
    for n in range(4):
        back[128 * n : 128 * n + 128] = dot(a[n], link[...], precision=HIGH)
    for copy in copies:
        copy.wait()
    summed = from_zl[0]
    for n in range(1, 8):
        summed = summed + from_zl[n]
    s_all[core, y, x] = summed[:48]
    w_sum = rows_of(summed[48:])
    copies = [start(s_all.at[core, y, x], s_all.at[core, y, x], peer(x=v)) for v in x_at]
    for n in (6, 7):
        loads[n].wait()
    v = w_sum - jnp.concatenate([rrhs_ref[...], jnp.zeros((6, 512), F32)])
    for n in range(4):
        v_blocks[n] = v[:, 128 * n : 128 * n + 128]
    for copy in copies:
        copy.wait()
    own_block = start(s_all.at[core, y], s_all.at[core, y], core_peer)
    other_blocks = [start(s_all.at[core, y], s_all.at[core, y], peer(y=v)) for v in y_at]

    turn = [y] + y_at

    def spot(t):
        return pl.ds(pl.multiple_of(128 * turn[t % 4], 128), 128)

    def place(t, q):
        block = jnp.concatenate([s_all[n // 4, turn[t], n % 4, 16 * q : 16 * q + 16] for n in range(8)])
        u = (t + q) % 4
        root[t, :, 128 * u : 128 * u + 128] = block + rdiag[spot(t), spot(u)]
        if q == 1:
            root[u, :, 128 * t : 128 * t + 128] = block.T + rdiag[spot(u), spot(t)]

    def between_root(k):
        if k == 0:
            forward = []
            for copy, v in zip(other_blocks, reversed(y_at)):
                copy.wait()
                forward.append(start(s_all.at[core, v], s_all.at[core, v], core_peer))
            place(0, 1)
            place(0, 2)
            for copy in forward:
                copy.wait()
            for t in range(1, 4):
                for q in range(3):
                    place(t, q)

    own_block.wait()
    place(0, 0)
    inverse_512(root, between_root)
    turned = dot(v_blocks[turn[0]], root[0], precision=HIGH)
    for t in range(1, 4):
        turned = turned + dot(v_blocks[turn[t]], root[t], precision=HIGH)
    for t in range(4):
        x_blocks[turn[t]] = turned[:, 128 * t : 128 * t + 128]
    root_sol = jnp.concatenate([x_blocks[n] for n in range(4)], axis=1)
    node_sol = solved[64:] - dot(root_sol, back[...], ((1,), (1,)), precision=HIGH)
    for n in range(16):
        x_rows[n] = node_sol[:2, 32 * n : 32 * n + 32]
    update = dot(node_sol.astype(BF16), reduced[...])
    difference = (update - projected[...]).astype(BF16)
    out_ref[0:2] = dot(difference, factor[...], ((1,), (1,)))[:2]
    out_ref[2:4, :512] = root_sol[:2]
    out_ref[4:6, :32] = x_rows[scen]


def parted(all_ref, leaf_ref, node_ref, root_ref):
    leaf_ref[...] = all_ref[0:2]
    root_ref[...] = all_ref[2:4, :512]
    node_ref[...] = all_ref[4:6, :32]


def local(factors, couple, leaf_rhs, node_diag, node_rhs, link_root, root_diag, root_rhs):
    vmem, hbm = pl.BlockSpec(memory_space=pltpu.VMEM), pl.BlockSpec(memory_space=pl.ANY)
    copies = 64
    everything = pl.pallas_call(
        body,
        out_shape=jax.ShapeDtypeStruct((8, 1024), F32),
        in_specs=[hbm] * 8,
        out_specs=vmem,
        scratch_shapes=[
            pltpu.VMEM((1024, 1024), BF16),
            pltpu.VMEM((1024, 512), BF16),
            pltpu.VMEM((2, 1024), BF16),
            pltpu.VMEM((32, 512), F32),
            pltpu.VMEM((2, 32), F32),
            pltpu.VMEM((32, 512), F32),
            pltpu.VMEM((512, 512), F32),
            pltpu.VMEM((2, 512), F32),
            pltpu.VMEM((512, 1024), BF16),
            pltpu.VMEM((8, 1024), F32),
            pltpu.VMEM((4, 512, 128), F32),
            pltpu.VMEM((2, 4, 16, 128), F32),
            pltpu.VMEM((2, 4, 16, 128), F32),
            pltpu.VMEM((2, 16, 128), F32),
            pltpu.VMEM((2, 4, 16, 128), F32),
            pltpu.VMEM((2, 4, 152, 128), F32),
            pltpu.VMEM((2, 4, 152, 128), F32),
            pltpu.VMEM((2, 152, 128), F32),
            pltpu.VMEM((2, 4, 152, 128), F32),
            pltpu.VMEM((512, 512), F32),
            pltpu.VMEM((128, 512), F32),
            pltpu.VMEM((4, 128, 512), F32),
            pltpu.VMEM((72, 512), F32),
            pltpu.VMEM((4, 64, 128), F32),
            pltpu.VMEM((4, 56, 128), F32),
            pltpu.VMEM((4, 56, 128), F32),
            pltpu.VMEM((8, 56, 128), F32),
            pltpu.VMEM((512, 512), F32),
            pltpu.VMEM((2, 4, 4, 48, 128), F32),
            pltpu.VMEM((4, 128, 512), F32),
            pltpu.VMEM((4, 8, 128), F32),
            pltpu.VMEM((4, 8, 128), F32),
            pltpu.VMEM((16, 2, 32), F32),
            pltpu.SemaphoreType.DMA((copies,)),
            pltpu.SemaphoreType.DMA((copies,)),
            pltpu.SemaphoreType.DMA((8,)),
        ],
        compiler_params=pltpu.CompilerParams(
            collective_id=0, has_side_effects=True, vmem_limit_bytes=60 * 1024 * 1024
        ),
        name="newton",
    )(factors[0, 0], couple[0, 0], leaf_rhs[0, 0], node_diag[0], node_rhs[0], link_root[0], root_diag, root_rhs)
    leaf, node, root = pl.pallas_call(
        parted,
        out_shape=(
            jax.ShapeDtypeStruct((2, 1024), F32),
            jax.ShapeDtypeStruct((2, 32), F32),
            jax.ShapeDtypeStruct((2, 512), F32),
        ),
        in_specs=[vmem],
        out_specs=(vmem, vmem, vmem),
        name="parted",
    )(everything)
    return (leaf[None, None], node[None], root)


def solution(mesh):
    torus = Mesh(mesh.devices.reshape(2, 4, 2, 4, 8), AXES)
    scen, node = ("zh", "y", "core"), ("x", "zl")
    placed = (
        P(node, scen, None, None),
        P(node, scen, None, None),
        P(node, scen, None, None),
        P(node, scen, None),
        P(node, None, scen),
        P(node, scen, None),
        P(),
        P(),
    )
    return jax.shard_map(
        local,
        mesh=torus,
        in_specs=placed,
        out_specs=(P(node, scen, None, None), P(node, None, scen), P()),
        check_vma=False,
    )
```

```python
import jax
import jax.numpy as jnp
from jax import lax
from jax.experimental import pallas as pl
from jax.experimental.pallas import tpu as pltpu
from jax.sharding import Mesh
from jax.sharding import PartitionSpec as P

AXES = ("zh", "y", "core", "x", "zl")
MESH = pl.DeviceIdType.MESH
HIGH = lax.Precision.HIGHEST
F32 = jnp.float32
BF16 = jnp.bfloat16


def dot(a, b, dims=((1,), (0,)), precision=None):
    return lax.dot_general(a, b, (dims, ((), ())), precision=precision, preferred_element_type=F32)


def thirds(v):
    high = v.astype(BF16).astype(F32)
    mid = (v - high).astype(BF16).astype(F32)
    return high, mid, v - high - mid


def inverse_128(a, work=()):
    rows = lax.broadcasted_iota(jnp.int32, (8, 128), 0)
    lanes = lax.broadcasted_iota(jnp.int32, (8, 128), 1)
    wide_lanes = lax.broadcasted_iota(jnp.int32, (128, 128), 1)
    work = list(work)
    following = a[:8]
    for s in range(16):
        at = 8 * s
        panel = following
        ah, am, al = thirds(jnp.where(lanes < at, -panel, panel))
        cols = jnp.stack([jnp.broadcast_to(panel[:, at + j : at + j + 1], (8, 128)) for j in range(8)])
        here = (lanes >= at) & (lanes < at + 8)
        panel = jnp.where(here, jnp.where(lanes - at == rows, 1.0, 0.0), panel)
        for j in range(8):
            mine = rows == j
            col = cols[0]
            inv = pl.reciprocal(jnp.broadcast_to(col[j : j + 1], (8, 128)), approx=True)
            f = jnp.where(mine, -inv, col * inv)
            if j < 7:
                rest = cols[1:]
                pivot = jnp.broadcast_to(rest[:, j : j + 1], rest.shape)
                cols = jnp.where(mine[None], 0.0, rest) - f[None] * pivot
            panel = jnp.where(mine, 0.0, panel) - f * jnp.broadcast_to(panel[j : j + 1], (8, 128))
        if s < 15:
            old = a[at + 8 : at + 16]
            following = jnp.where(here, 0.0, old)
            for j in range(8):
                following = following - jnp.broadcast_to(old[:, at + j : at + j + 1], (8, 128)) * jnp.broadcast_to(
                    panel[j : j + 1], (8, 128)
                )
        bh, bm, bl = thirds(panel)
        left = jnp.concatenate([ah, ah, ah, am, am, al]).astype(BF16)
        right = jnp.concatenate([bh, bm, bl, bh, bm, bh]).astype(BF16)
        new = jnp.where((wide_lanes >= at) & (wide_lanes < at + 8), 0.0, a) - dot(left, right, ((0,), (0,)))
        a = jnp.concatenate([part for part in (new[:at], panel, new[at + 8 :]) if part.shape[0]])
        for _ in range(-(-len(work) // (16 - s))):
            work.pop(0)()
    return a


def inverse_512(a, between=None, finish=True):
    work = []
    cols = [slice(128 * n, 128 * n + 128) for n in range(4)]
    for k in range(4):
        inv = inverse_128(a[k, :, cols[k]], work)
        if between is not None:
            between(k)
        if k == 3 and not finish:
            return inv
        work = []
        nxt = k + 1
        def row(j, k=k, inv=inv):
            a[k, :, cols[j]] = dot(inv, a[k, :, cols[j]], precision=HIGH)
        def update(i, j, k=k):
            a[i, :, cols[j]] = a[i, :, cols[j]] - dot(a[i, :, cols[k]], a[k, :, cols[j]], precision=HIGH)
        def column(i, k=k, inv=inv):
            a[i, :, cols[k]] = -dot(a[i, :, cols[k]], inv, precision=HIGH)
        others = [n for n in range(4) if n != k]
        if nxt < 4:
            row(nxt); update(nxt, nxt)
        for j in others:
            if j != nxt: work.append(lambda j=j, f=row: f(j))
        for j in others:
            for i in others:
                if not (i == j == nxt): work.append(lambda i=i, j=j, f=update: f(i, j))
        for i in others: work.append(lambda i=i, f=column: f(i))
        def keep(k=k, inv=inv):
            a[k, :, cols[k]] = inv

        work.append(keep)
    for w in work:
        w()


def tile_of(vec):
    return jnp.concatenate([vec[:, 128 * j : 128 * j + 128] for j in range(4)])


def rows_of(tile):
    vec = jnp.concatenate([tile[2 * j : 2 * j + 2] for j in range(4)], axis=1)
    return jnp.concatenate([vec, jnp.zeros((6, 512), F32)])


def body(
    factor_hbm, couple_hbm, rights_hbm, diag_hbm, nrhs_hbm, link_hbm, rdiag_hbm, rrhs_hbm,
    out_ref,
    factor, coupling, rights_ref, diag_ref, nrhs_ref, link_ref, rdiag, rrhs_ref, reduced, projected, part, first, first_from, first_z, first_sum,
    rest, rest_from, rest_z, rest_sum, link, link_t, a, left, e_blocks, e_part, from_x, from_zl, back, s_all, root, v_blocks, x_blocks, x_rows,
    send, recv, load,
):
    zh, y, core, x, zl = (lax.axis_index(n) for n in AXES)
    scen = zh * 8 + y * 2 + core

    def peer(**at):
        here = dict(zh=zh, y=y, core=core, x=x, zl=zl)
        here.update(at)
        return tuple(here[n] for n in AXES)

    z_peer, core_peer = peer(zh=1 - zh), peer(core=1 - core)
    y_at = [lax.rem(y + d, 4) for d in range(1, 4)]
    x_at = [lax.rem(x + d, 4) for d in range(1, 4)]
    zl_at = [lax.rem(zl + d, 8) for d in range(1, 8)]
    peers = [z_peer, core_peer] + [peer(y=v) for v in y_at] + [peer(x=v) for v in x_at] + [peer(zl=v) for v in zl_at]
    barrier = pltpu.get_barrier_semaphore()
    for device in peers:
        pl.semaphore_signal(barrier, 1, device_id=device, device_id_type=MESH)

    loads = [
        pltpu.make_async_copy(src, dst, load.at[n])
        for n, (src, dst) in enumerate(
            (
                (couple_hbm, coupling),
                (factor_hbm, factor),
                (rights_hbm, rights_ref),
                (diag_hbm, diag_ref),
                (nrhs_hbm, nrhs_ref),
                (link_hbm, link_ref),
                (rdiag_hbm, rdiag),
                (rrhs_hbm, rrhs_ref),
            )
        )
    ]
    for copy in loads:
        copy.start()

    used = [0]

    def start(src, dst, device):
        n = used[0]
        used[0] += 1
        copy = pltpu.make_async_remote_copy(
            src_ref=src, dst_ref=dst, send_sem=send.at[n], recv_sem=recv.at[n], device_id=device, device_id_type=MESH
        )
        copy.start()
        return copy

    for n in range(6):
        loads[n].wait()
    rights = jnp.concatenate([rights_ref[...].astype(F32), jnp.zeros((6, 1024), F32)]).astype(BF16)
    reduced[...] = dot(coupling[...], factor[...], ((0,), (0,))).astype(BF16)
    projected[...] = dot(rights, factor[...])
    for j in range(4):
        part[j, 128 * j :] = dot(reduced[128 * j :], reduced[128 * j : 128 * j + 128], ((1,), (1,)))
    low = projected[...].astype(BF16)
    vec = dot(low, reduced[...], ((1,), (1,)))
    own = pl.ds(pl.multiple_of(32 * scen, 32), 32)
    for j in range(4):
        part[j, own] = part[j, own] + diag_ref[:, 128 * j : 128 * j + 128]
    rows = lax.broadcasted_iota(jnp.int32, (8, 128), 0)
    lanes = lax.broadcasted_iota(jnp.int32, (8, 128), 1)
    strip = jnp.concatenate([nrhs_ref[...]] * 4, axis=1)
    strip = jnp.concatenate([strip] * 4)
    mine = (rows // 2 == scen // 4) & (lanes // 32 == lax.rem(scen, 4))
    vec_tile = tile_of(vec[:2]) + jnp.where(mine, strip, 0.0)
    for c in range(2):
        for v in range(4):
            p = 4 * c + v
            first[c, v] = part[0, 16 * p : 16 * p + 16]
            rest[c, v, 0:48] = part[0, 128 + 48 * p : 176 + 48 * p]
            rest[c, v, 48:96] = part[1, 128 + 48 * p : 176 + 48 * p]
            rest[c, v, 96:128] = part[2, 256 + 32 * p : 288 + 32 * p]
            rest[c, v, 128:144] = part[3, 384 + 16 * p : 400 + 16 * p]
            rest[c, v, 144:152] = vec_tile

    pl.semaphore_wait(barrier, len(peers))

    first_core = start(first.at[1 - core], first_from.at[0], core_peer)
    rest_core = start(rest.at[1 - core], rest_from.at[0], core_peer)
    first_core.wait()
    first[core] = first[core] + first_from[0]
    first_y = [start(first.at[core, v], first_from.at[1, d], peer(y=v)) for d, v in enumerate(y_at)]
    rest_core.wait()
    rest[core] = rest[core] + rest_from[0]
    rest_y = [start(rest.at[core, v], rest_from.at[1, d], peer(y=v)) for d, v in enumerate(y_at)]
    for copy in first_y:
        copy.wait()
    first_z[0] = (first[core, y] + first_from[1, 0]) + (first_from[1, 1] + first_from[1, 2])
    first_far = start(first_z.at[0], first_z.at[1], z_peer)
    for copy in rest_y:
        copy.wait()
    rest_z[0] = (rest[core, y] + rest_from[1, 0]) + (rest_from[1, 1] + rest_from[1, 2])
    rest_far = start(rest_z.at[0], rest_z.at[1], z_peer)

    first_far.wait()
    first_sum[core, y] = first_z[0] + first_z[1]
    first_y = [start(first_sum.at[core, y], first_sum.at[core, y], peer(y=v)) for v in y_at]
    for copy in first_y:
        copy.wait()
    first_core = start(first_sum.at[core], first_sum.at[core], core_peer)
    rest_far.wait()
    rest_sum[core, y] = rest_z[0] + rest_z[1]
    rest_y = [start(rest_sum.at[core, y], rest_sum.at[core, y], peer(y=v)) for v in y_at]
    rest_core = [start(rest_sum.at[core, y], rest_sum.at[core, y], core_peer)]
    link[own] = link_ref[...]
    link_far = start(link_ref, link.at[own], z_peer)
    first_core.wait()
    a[0, :, :128] = jnp.concatenate([first_sum[p // 4, p % 4] for p in range(8)])
    later = {}

    def between(k):
        if k == 0:
            for copy, v in zip(rest_y, reversed(y_at)):
                copy.wait()
                rest_core.append(start(rest_sum.at[core, v], rest_sum.at[core, v], core_peer))
            later["own"] = [start(link_ref, link.at[own], peer(y=v)) for v in y_at]
            for copy in rest_core:
                copy.wait()
            spans = ((0, 1, 0, 48), (1, 1, 48, 48), (2, 2, 96, 32), (3, 3, 128, 16))
            for j, i0, low_row, n in spans:
                column = jnp.concatenate([rest_sum[p // 4, p % 4, low_row : low_row + n] for p in range(8)])
                for i in range(i0, 4):
                    block = column[128 * (i - i0) : 128 * (i - i0) + 128]
                    a[i, :, 128 * j : 128 * j + 128] = block
                    if i > j:
                        a[j, :, 128 * i : 128 * i + 128] = block.T
        if k == 1:
            link_far.wait()
            for copy in later["own"]:
                copy.wait()
            far = pl.ds(pl.multiple_of(32 * ((1 - zh) * 8 + y * 2 + core), 32), 32)
            later["near"] = [start(link.at[far], link.at[far], peer(y=v)) for v in y_at]
        if k == 2:
            for copy in later["near"]:
                copy.wait()
            later["core"] = []
            for n in range(8):
                at = pl.ds(pl.multiple_of(32 * (2 * n + core), 32), 32)
                later["core"].append(start(link.at[at], link.at[at], core_peer))

    inverse_512(a, between)
    for copy in later["core"]:
        copy.wait()
    vec_total = rest_sum[core, y, 144:]

    band = pl.ds(pl.multiple_of(128 * y, 128), 128)
    for n in range(4):
        link_t[:, 128 * n : 128 * n + 128] = link[128 * n : 128 * n + 128, band].T
    z_rows = rows_of(vec_total)
    left[:64] = link_t[pl.ds(pl.multiple_of(64 * core, 64), 64)]
    left[64:] = z_rows

    def by_inverse(v):
        out = dot(v[:, :128], a[0], precision=HIGH)
        for n in range(1, 4):
            out = out + dot(v[:, 128 * n : 128 * n + 128], a[n], precision=HIGH)
        return out

    solved = by_inverse(left[...])
    e_rows = dot(solved, link[...], precision=HIGH)
    w_tile = tile_of(e_rows[64:66])
    for n in range(4):
        e_blocks[n] = e_rows[:64, 128 * n : 128 * n + 128]
    for q in range(3):
        block = e_blocks[lax.rem(y + q, 4)]
        for n in range(4):
            e_part[n, 16 * q : 16 * q + 16] = block[16 * n : 16 * n + 16]
    for n in range(4):
        e_part[n, 48:] = w_tile

    from_x[x] = e_part[x]
    copies = [start(e_part.at[v], from_x.at[x], peer(x=v)) for v in x_at]
    for copy in copies:
        copy.wait()
    from_zl[zl] = (from_x[0] + from_x[1]) + (from_x[2] + from_x[3])
    copies = [start(from_zl.at[zl], from_zl.at[zl], peer(zl=v)) for v in zl_at]
    for n in range(4):
        back[128 * n : 128 * n + 128] = dot(a[n], link[...], precision=HIGH)
    for copy in copies:
        copy.wait()
    summed = from_zl[0]
    for n in range(1, 8):
        summed = summed + from_zl[n]
    s_all[core, y, x] = summed[:48]
    w_sum = rows_of(summed[48:])
    copies = [start(s_all.at[core, y, x], s_all.at[core, y, x], peer(x=v)) for v in x_at]
    for n in (6, 7):
        loads[n].wait()
    v = w_sum - jnp.concatenate([rrhs_ref[...], jnp.zeros((6, 512), F32)])
    for n in range(4):
        v_blocks[n] = v[:, 128 * n : 128 * n + 128]
    for copy in copies:
        copy.wait()
    own_block = start(s_all.at[core, y], s_all.at[core, y], core_peer)
    other_blocks = [start(s_all.at[core, y], s_all.at[core, y], peer(y=v)) for v in y_at]

    turn = [y] + y_at

    def spot(t):
        return pl.ds(pl.multiple_of(128 * turn[t % 4], 128), 128)

    def place(t, q):
        block = jnp.concatenate([s_all[n // 4, turn[t], n % 4, 16 * q : 16 * q + 16] for n in range(8)])
        u = (t + q) % 4
        root[t, :, 128 * u : 128 * u + 128] = block + rdiag[spot(t), spot(u)]
        if q == 1:
            root[u, :, 128 * t : 128 * t + 128] = block.T + rdiag[spot(u), spot(t)]

    def between_root(k):
        if k == 0:
            forward = []
            for copy, v in zip(other_blocks, reversed(y_at)):
                copy.wait()
                forward.append(start(s_all.at[core, v], s_all.at[core, v], core_peer))
            place(0, 1)
            place(0, 2)
            for copy in forward:
                copy.wait()
            for t in range(1, 4):
                for q in range(3):
                    place(t, q)

    own_block.wait()
    place(0, 0)
    last = inverse_512(root, between_root, finish=False)
    turned = dot(v_blocks[turn[0]], root[0], precision=HIGH)
    for t in range(1, 3):
        turned = turned + dot(v_blocks[turn[t]], root[t], precision=HIGH)
    x_last = dot(v_blocks[turn[3]] - turned[:, 384:], last, precision=HIGH)
    turned = jnp.concatenate([turned[:, :384] + dot(x_last, root[3, :, :384], precision=HIGH), x_last], axis=1)
    for t in range(4):
        x_blocks[turn[t]] = turned[:, 128 * t : 128 * t + 128]
    root_sol = jnp.concatenate([x_blocks[n] for n in range(4)], axis=1)
    node_sol = solved[64:] - dot(root_sol, back[...], ((1,), (1,)), precision=HIGH)
    for n in range(16):
        x_rows[n] = node_sol[:2, 32 * n : 32 * n + 32]
    update = dot(node_sol.astype(BF16), reduced[...])
    difference = (update - projected[...]).astype(BF16)
    out_ref[0:2] = dot(difference, factor[...], ((1,), (1,)))[:2]
    out_ref[2:4, :512] = root_sol[:2]
    out_ref[4:6, :32] = x_rows[scen]


def parted(all_ref, leaf_ref, node_ref, root_ref):
    leaf_ref[...] = all_ref[0:2]
    root_ref[...] = all_ref[2:4, :512]
    node_ref[...] = all_ref[4:6, :32]


def local(factors, couple, leaf_rhs, node_diag, node_rhs, link_root, root_diag, root_rhs):
    vmem, hbm = pl.BlockSpec(memory_space=pltpu.VMEM), pl.BlockSpec(memory_space=pl.ANY)
    copies = 64
    everything = pl.pallas_call(
        body,
        out_shape=jax.ShapeDtypeStruct((8, 1024), F32),
        in_specs=[hbm] * 8,
        out_specs=vmem,
        scratch_shapes=[
            pltpu.VMEM((1024, 1024), BF16),
            pltpu.VMEM((1024, 512), BF16),
            pltpu.VMEM((2, 1024), BF16),
            pltpu.VMEM((32, 512), F32),
            pltpu.VMEM((2, 32), F32),
            pltpu.VMEM((32, 512), F32),
            pltpu.VMEM((512, 512), F32),
            pltpu.VMEM((2, 512), F32),
            pltpu.VMEM((512, 1024), BF16),
            pltpu.VMEM((8, 1024), F32),
            pltpu.VMEM((4, 512, 128), F32),
            pltpu.VMEM((2, 4, 16, 128), F32),
            pltpu.VMEM((2, 4, 16, 128), F32),
            pltpu.VMEM((2, 16, 128), F32),
            pltpu.VMEM((2, 4, 16, 128), F32),
            pltpu.VMEM((2, 4, 152, 128), F32),
            pltpu.VMEM((2, 4, 152, 128), F32),
            pltpu.VMEM((2, 152, 128), F32),
            pltpu.VMEM((2, 4, 152, 128), F32),
            pltpu.VMEM((512, 512), F32),
            pltpu.VMEM((128, 512), F32),
            pltpu.VMEM((4, 128, 512), F32),
            pltpu.VMEM((72, 512), F32),
            pltpu.VMEM((4, 64, 128), F32),
            pltpu.VMEM((4, 56, 128), F32),
            pltpu.VMEM((4, 56, 128), F32),
            pltpu.VMEM((8, 56, 128), F32),
            pltpu.VMEM((512, 512), F32),
            pltpu.VMEM((2, 4, 4, 48, 128), F32),
            pltpu.VMEM((4, 128, 512), F32),
            pltpu.VMEM((4, 8, 128), F32),
            pltpu.VMEM((4, 8, 128), F32),
            pltpu.VMEM((16, 2, 32), F32),
            pltpu.SemaphoreType.DMA((copies,)),
            pltpu.SemaphoreType.DMA((copies,)),
            pltpu.SemaphoreType.DMA((8,)),
        ],
        compiler_params=pltpu.CompilerParams(
            collective_id=0, has_side_effects=True, vmem_limit_bytes=60 * 1024 * 1024
        ),
        name="newton",
    )(factors[0, 0], couple[0, 0], leaf_rhs[0, 0], node_diag[0], node_rhs[0], link_root[0], root_diag, root_rhs)
    leaf, node, root = pl.pallas_call(
        parted,
        out_shape=(
            jax.ShapeDtypeStruct((2, 1024), F32),
            jax.ShapeDtypeStruct((2, 32), F32),
            jax.ShapeDtypeStruct((2, 512), F32),
        ),
        in_specs=[vmem],
        out_specs=(vmem, vmem, vmem),
        name="parted",
    )(everything)
    return (leaf[None, None], node[None], root)


def solution(mesh):
    torus = Mesh(mesh.devices.reshape(2, 4, 2, 4, 8), AXES)
    scen, node = ("zh", "y", "core"), ("x", "zl")
    placed = (
        P(node, scen, None, None),
        P(node, scen, None, None),
        P(node, scen, None, None),
        P(node, scen, None),
        P(node, None, scen),
        P(node, scen, None),
        P(),
        P(),
    )
    return jax.shard_map(
        local,
        mesh=torus,
        in_specs=placed,
        out_specs=(P(node, scen, None, None), P(node, None, scen), P()),
        check_vma=False,
    )
```
